512 devices in a mesh: context: 32 (over y, z_lo, core), tensor: 16 (over x, z_hi).
Axes of the slice: x: 4, y: 8, z: 8 (z_hi: 4, z_lo: 2; z = z_hi * 2 + z_lo), core: 2. Of those that a mesh axis runs over, the one named last changes fastest.
Arguments:
- block_input: bfloat16 [4096, 8192], P(('context', 'tensor')), may hold values from -2 to 2
- norm_scale_weight: float32 [8192], replicated, may hold values from 0.1 to 1.9
- kv_weight: bfloat16 [8192, 2048], P('context', 'tensor'), may hold values from -0.0625 to 0.0625
- q_weight: bfloat16 [8192, 4096], P('context', 'tensor'), may hold values from -0.0625 to 0.0625
- kv_cotangent: bfloat16 [4096, 16, 256], P('context', 'tensor'), may hold values from -0.09375 to 0.09375
- q_cotangent: bfloat16 [4096, 4096], P('context', 'tensor'), may hold values from -0.09375 to 0.09375
Outputs:
- input_gradient: bfloat16 [4096, 8192], P(('context', 'tensor'))
- grad_weight: float32 [8192, 2048], P('context', 'tensor')
- grad_q_weight: float32 [8192, 4096], P('context', 'tensor')
The draws below stay inside these ranges and needn't reach their ends.
All inputs are finite; a program needn't handle non-finite values.
Results may differ from the reference program's by a relative error of at most 0.019.
Values may be sent and summed in bfloat16 or wider, within the bound.
A program may use at most 64 MiB of HBM per device.

```python
import math
import jax
import jax.numpy as jnp
from jax import lax

D = 8192
HEAD = 128
QH_DEV = 2
TOKENS = 4096
N_TENSOR = 16


def draw_block_input(key, part):
    key = jax.random.fold_in(key, 11)
    key_values, key_rows, key_cols = jax.random.split(key, 3)
    values = jnp.clip(jax.random.normal(key_values, (TOKENS, D), jnp.float32), -4.0, 4.0)
    row_scale = jnp.exp(jax.random.uniform(key_rows, (TOKENS, 1), jnp.float32) * math.log(10.0))
    col_scale = jnp.exp(jax.random.uniform(key_cols, (1, D), jnp.float32) * math.log(10.0))
    return (0.005 * values * row_scale * col_scale).astype(jnp.bfloat16)


def steps_of(own_key, extent, cuts, smallest, top_value):
    gain = 1.0
    for axis_at, shards_of in cuts:
        steps = jax.random.uniform(jax.random.fold_in(jax.random.fold_in(own_key, 6), axis_at), (shards_of,), jnp.float32, smallest / len(cuts), top_value / len(cuts))
        gain = gain * jnp.repeat(jnp.exp(steps), extent[axis_at] // shards_of).reshape((-1,) + (1,) * (len(extent) - 1 - axis_at))
    return gain


def gaussian(key, dims, scale, bound, shards=(), dtype=jnp.bfloat16):
    values = jax.random.normal(key, dims, jnp.float32) * scale
    if len(shards) > 0:
        values = steps_of(key, dims, shards, -0.22, 0.18) * values
    return jnp.clip(values, min=-bound, max=bound).astype(dtype)


def setup_inputs(seed: int = 0) -> dict:
    seeds = jax.random.split(jax.random.key(seed), 7)
    block_input = draw_block_input(jax.random.fold_in(seeds[6], 71), 0)
    norm_scale_weight = jnp.clip(1.0 + 0.18 * jax.random.normal(seeds[1], (D,), jnp.float32), 0.1, 1.9)
    kv_weight = gaussian(seeds[2], (D, N_TENSOR * HEAD), D ** -0.5, 0.0625, ((0, 32), (1, 16)))
    q_weight = gaussian(seeds[3], (D, N_TENSOR * QH_DEV * HEAD), D ** -0.5, 0.0625, ((0, 32), (1, 16)))
    kv_cotangent = gaussian(seeds[4], (TOKENS, N_TENSOR, 2 * HEAD), TOKENS ** -0.5, 0.09375, ((0, 32), (1, 16)))
    q_cotangent = gaussian(seeds[5], (TOKENS, N_TENSOR * QH_DEV * HEAD), TOKENS ** -0.5, 0.09375, ((0, 32), (1, 16)))
    return dict(block_input=block_input, norm_scale_weight=norm_scale_weight, kv_weight=kv_weight, q_weight=q_weight, kv_cotangent=kv_cotangent, q_cotangent=q_cotangent)


def reference(block_input, norm_scale_weight, kv_weight, q_weight, kv_cotangent, q_cotangent):
    input_single32 = block_input.astype(jnp.float32)
    inverse_root_scale = lax.rsqrt(lax.optimization_barrier(jnp.mean(input_single32 * input_single32, axis=-1, keepdims=True)) + 1e-06)
    unit_input_rows = input_single32 * inverse_root_scale
    normalized_rows = (unit_input_rows * norm_scale_weight).astype(jnp.bfloat16)
    cotangent = kv_cotangent.astype(jnp.float32).reshape(TOKENS, N_TENSOR // 2, 2, 2 * HEAD)
    paired = (cotangent[:, :, 0, :] + cotangent[:, :, 1, :]).astype(jnp.bfloat16)
    block_grad = paired.reshape(TOKENS, N_TENSOR, HEAD)
    grad_weight = jnp.dot(normalized_rows.T, block_grad.reshape(TOKENS, N_TENSOR * HEAD), preferred_element_type=jnp.float32)
    grad_q_weight = jnp.dot(normalized_rows.T, q_cotangent, preferred_element_type=jnp.float32)
    stacked_grad = jnp.transpose(block_grad, (1, 0, 2))
    stacked_weight = jnp.transpose(kv_weight.reshape(D, N_TENSOR, HEAD), (1, 0, 2))
    stacked_qgrad = jnp.transpose(q_cotangent.reshape(TOKENS, N_TENSOR, QH_DEV * HEAD), (1, 0, 2))
    stacked_qweight = jnp.transpose(q_weight.reshape(D, N_TENSOR, QH_DEV * HEAD), (1, 0, 2))

    def accumulate(running, operands):
        grad_part, weight_part, qgrad_part, qweight_part = operands
        term = lax.dot_general(grad_part, weight_part, (((1,), (1,)), ((), ())), preferred_element_type=jnp.float32)
        term = term + lax.dot_general(qgrad_part, qweight_part, (((1,), (1,)), ((), ())), preferred_element_type=jnp.float32)
        return (running + term.astype(jnp.bfloat16).astype(jnp.float32), None)
    normed_grad, unused = lax.scan(accumulate, jnp.zeros((TOKENS, D), jnp.float32), (stacked_grad, stacked_weight, stacked_qgrad, stacked_qweight))
    gain_scaled_rows = norm_scale_weight * normed_grad
    input_gradient = inverse_root_scale * (gain_scaled_rows - unit_input_rows * lax.optimization_barrier(jnp.mean(gain_scaled_rows * unit_input_rows, axis=-1, keepdims=True)))
    return (input_gradient.astype(jnp.bfloat16), grad_weight, grad_q_weight)
```

```python
import jax
import jax.numpy as jnp
from jax import lax
from jax.sharding import PartitionSpec as P


def partner_2(value, axis, bit):
    return lax.ppermute(value, axis, [(i, i ^ 1 << bit) for i in range(lax.axis_size(axis))])


def on_device(block_input, norm_scale_weight, kv_weight, q_weight, kv_cotangent, q_cotangent):
    n_context = lax.axis_size("context")
    n_tensor = lax.axis_size("tensor")
    own, features = block_input.shape
    depth = features // n_context
    rows32 = block_input.astype(jnp.float32)
    inv = lax.rsqrt(jnp.mean(rows32 * rows32, axis=-1, keepdims=True) + 1e-06)
    unit = rows32 * inv
    normed = (unit * norm_scale_weight).astype(jnp.bfloat16)
    spread = lax.all_to_all(
        normed.reshape(own, n_context, depth).transpose(1, 0, 2), "context", split_axis=0, concat_axis=0, tiled=True
    )
    gathered = lax.all_gather(spread, "tensor", axis=1)
    tokens = gathered.reshape(n_context * n_tensor * own, depth)
    width = kv_weight.shape[1]
    parity = lax.axis_index("tensor") % 2
    cotangent = kv_cotangent[:, 0, :]
    keys_part = cotangent[:, :width]
    values_part = cotangent[:, width:]
    mine = jnp.where(parity == 0, keys_part, values_part)
    other = partner_2(jnp.where(parity == 0, values_part, keys_part), "tensor", 0)
    head_grad = (mine.astype(jnp.float32) + other.astype(jnp.float32)).astype(jnp.bfloat16)
    joint_grad = jnp.concatenate([head_grad, q_cotangent], axis=1)
    joint_weight = jnp.concatenate([kv_weight, q_weight], axis=1)
    all_grad = lax.all_gather(joint_grad, "context", axis=0, tiled=True)
    partials = lax.dot_general(
        all_grad, joint_weight, (((1,), (1,)), ((), ())), preferred_element_type=jnp.float32
    ).astype(jnp.bfloat16)
    partials = partials.reshape(n_context, n_tensor, own, depth)
    summed = lax.psum_scatter(partials, "tensor", scatter_dimension=1, tiled=False)
    back = lax.all_to_all(summed, "context", split_axis=0, concat_axis=0, tiled=True)
    normed_grad = back.transpose(1, 0, 2).reshape(own, features).astype(jnp.float32)
    scaled = norm_scale_weight * normed_grad
    input_gradient = inv * (scaled - unit * jnp.mean(scaled * unit, axis=-1, keepdims=True))
    joint_result = lax.dot_general(
        tokens, all_grad, (((0,), (0,)), ((), ())), preferred_element_type=jnp.float32
    )
    return (input_gradient.astype(jnp.bfloat16), joint_result[:, :width], joint_result[:, width:])


def solution(mesh):
    in_specs = (
        P(("context", "tensor"), None),
        P(),
        P("context", "tensor"),
        P("context", "tensor"),
        P("context", "tensor", None),
        P("context", "tensor"),
    )
    out_specs = (P(("context", "tensor"), None), P("context", "tensor"), P("context", "tensor"))
    return jax.shard_map(
        on_device, mesh=mesh, in_specs=in_specs, out_specs=out_specs, check_vma=False
    )
```

```python
import jax
import jax.numpy as jnp
from jax import lax
from jax.experimental import pallas as pl
from jax.experimental.pallas import tpu as pltpu
from jax.sharding import PartitionSpec as P

NY, NZL, NK = 8, 2, 2
NX, NZH = 4, 4
F32, BF16 = jnp.float32, jnp.bfloat16
N_COPIES = 105


def kernel(
    x_ref, gain_ref, kvw_ref, qw_ref, kvc_ref, qc_ref,
    dx_ref, gkv_ref, gq_ref,
    xk_keep, xk_send, xk_recv, xb, xg, xt,
    wb, kv_send, kv_recv, gs, gb,
    pb, pr, fb, fr, fk_keep, fk_send, fk_recv,
    gwp, gw_own, gw1, gw2, gws,
    send_sems, recv_sems,
):
    context = lax.axis_index("context")
    tensor = lax.axis_index("tensor")
    y, zl, k = lax.div(context, NZL * NK), lax.rem(lax.div(context, NK), NZL), lax.rem(context, NK)
    x, zh = lax.div(tensor, NZH), lax.rem(tensor, NZH)
    ozl, ok = 1 - zl, 1 - k

    def at_y(step):
        return lax.rem(y + (step + NY) % NY, NY)

    def at_x(step):
        return lax.rem(x + (step + NX) % NX, NX)

    def at_zh(step):
        return lax.rem(zh + (step + NZH) % NZH, NZH)

    def dev(yy=y, zz=zl, kk=k, xx=x, hh=zh):
        return {"context": (yy * NZL + zz) * NK + kk, "tensor": xx * NZH + hh}

    zls = (zl, ozl)
    far = [(s, o) for s in range(NY) for o in range(2) if (s, o) != (0, 0)]
    core_peer = dev(kk=ok)
    right, left = dev(yy=at_y(1)), dev(yy=at_y(-1))

    names = {}
    pending = []

    def number(name):
        return names.setdefault(name, len(names))

    def send(name, src, dst, to):
        slot = number(name)
        pltpu.make_async_remote_copy(
            src_ref=src, dst_ref=dst, send_sem=send_sems.at[slot], recv_sem=recv_sems.at[slot],
            device_id=to, device_id_type=pl.DeviceIdType.MESH,
        ).start()
        pending.append((src, slot))

    def arrived(name, dst):
        pltpu.make_async_copy(dst, dst, recv_sems.at[number(name)]).wait()

    peers = [core_peer]
    peers += [dev(yy=at_y(s), zz=zls[o]) for s, o in far]
    peers += [dev(xx=at_x(s)) for s in range(1, NX)]
    peers += [dev(hh=at_zh(s)) for s in range(1, NZH)]
    barrier = pltpu.get_barrier_semaphore()
    for peer in peers:
        pl.semaphore_signal(barrier, inc=1, device_id=peer, device_id_type=pl.DeviceIdType.MESH)

    parity = lax.rem(zh, 2)
    kvc = kvc_ref[...].astype(F32)
    keys, values = kvc[:, :128], kvc[:, 128:]
    kv_send[...] = jnp.where(parity == 0, values, keys).astype(BF16)
    pl.semaphore_wait(barrier, len(peers))

    send("kv", kv_send, kv_recv, dev(hh=zh + 1 - 2 * parity))

    rows = x_ref[...].astype(F32)
    inv = lax.rsqrt(jnp.mean(rows * rows, axis=-1, keepdims=True) + 1e-06)
    for b in range(NY * NZL):
        both = []
        for j in (0, 1):
            cols = slice((2 * b + j) * 256, (2 * b + j + 1) * 256)
            both.append((rows[:, cols] * inv * gain_ref[:, cols]).astype(BF16).astype(F32))
        xk_keep[b] = jnp.where(k == 0, both[0], both[1])
        xk_send[b] = jnp.where(k == 0, both[1], both[0])
    send("xk", xk_send, xk_recv, core_peer)

    arrived("kv", kv_recv)
    head = (jnp.where(parity == 0, keys, values) + kv_recv[...].astype(F32)).astype(BF16)
    for j in range(NX):
        gs[j, :, :128] = head[32 * j:32 * j + 32]
        gs[j, :, 128:] = qc_ref[32 * j:32 * j + 32, :]
    for s in (2, 1, 3):
        send(("ga", s), gs.at[at_x(s)], gb.at[y, k, zl, x], dev(xx=at_x(s)))
    gb[y, k, zl, x] = gs[x]

    wb[x, :, :128] = kvw_ref[...]
    wb[x, :, 128:] = qw_ref[...]
    send("w_right", wb.at[x], wb.at[x], dev(xx=at_x(1)))
    send("w_left", wb.at[x], wb.at[x], dev(xx=at_x(-1)))

    arrived("xk", xk_recv)
    for b in range(NY * NZL):
        keep, recv = xk_keep[b], xk_recv[b]
        pair = [jnp.where(k == 0, keep, recv), jnp.where(k == 0, recv, keep)]
        xb[b] = jnp.concatenate(pair, axis=0).astype(BF16)
    for s, o in far:
        send(("xa", s, o), xb.at[at_y(s) * NZL + zls[o]], xg.at[zh, y, zl], dev(yy=at_y(s), zz=zls[o]))
    xg[zh, y, zl] = xb[y * NZL + zl]

    for s in (1, 2, 3):
        arrived(("ga", s), gb.at[y, k, zl, at_x(-s)])

    def block(step, o):
        return gb.at[at_y(step), k, zls[o]]

    def ring_right(hop, o):
        send(("gr", hop, o), block(1 - hop, o), block(1 - hop, o), right)

    def ring_left(hop, o):
        send(("gl", hop, o), block(hop - 1, o), block(hop - 1, o), left)

    def to_core(step, o):
        send(("gk", step, o), block(step, o), block(step, o), core_peer)

    ring_right(1, 0)
    ring_left(1, 0)
    send("gz", block(0, 0), block(0, 0), dev(zz=ozl))
    to_core(0, 0)

    def normed_grad_terms(step):
        yy = at_y(step)
        for o in (0, 1):
            arrived(("gk", step, o), gb.at[yy, ok, zls[o]])
        acc = jnp.zeros((128, 256), F32)
        for j in range(NX):
            acc += lax.dot_general(
                gb[yy, :, :, j].reshape(128, 384), wb[j], (((1,), (1,)), ((), ())), preferred_element_type=F32
            )
        for h in range(NZH):
            for z in range(NZL):
                start = z * 32 + h * 8
                pb[yy, h, z] = jnp.concatenate([acc[start:start + 8], acc[64 + start:72 + start]], axis=0).astype(BF16)
        for s in (2, 1, 3):
            send(("p", step, s), pb.at[yy, at_zh(s)], pr.at[yy, zh], dev(hh=at_zh(s)))

    def normed_grad_sum(step):
        yy = at_y(step)
        for s in (1, 2, 3):
            arrived(("p", step, s), pr.at[yy, at_zh(-s)])
        total = pb[yy, zh].astype(F32)
        for s in (1, 2, 3):
            total += pr[yy, at_zh(s)].astype(F32)
        fb[yy] = total.astype(BF16)
        for o in (0, 1):
            if (step, o) != (0, 0):
                send(("f", step % NY, o), fb.at[yy, zls[o]], fr.at[y, zl], dev(yy=yy, zz=zls[o]))
        if step == 0:
            fr[y, zl] = fb[y, zl]

    arrived("gz", block(0, 1))
    ring_right(1, 1)
    ring_left(1, 1)
    to_core(0, 1)

    for s, o in far:
        arrived(("xa", s, o), xg.at[zh, at_y(-s), zls[o]])
    send("x_right", xg.at[zh], xg.at[zh], dev(hh=at_zh(1)))
    send("x_left", xg.at[zh], xg.at[zh], dev(hh=at_zh(-1)))

    arrived("w_right", wb.at[at_x(-1)])
    part = wb.at[at_x(-1), pl.ds(0, 128)]
    send("w_far0", part, part, dev(xx=at_x(1)))
    arrived("w_left", wb.at[at_x(1)])
    part = wb.at[at_x(1), pl.ds(128, 128)]
    send("w_far1", part, part, dev(xx=at_x(-1)))

    def hop_arrivals(hop):
        for o in (0, 1):
            if hop < 4 or o == 0:
                arrived(("gr", hop, o), block(-hop, o))
                if hop + 1 < 4 or (hop + 1 == 4 and o == 0):
                    ring_right(hop + 1, o)
                to_core(-hop if hop < 4 else 4, o)
            if hop < 4 or o == 1:
                arrived(("gl", hop, o), block(hop, o))
                if hop + 1 < 4 or (hop + 1 == 4 and o == 1):
                    ring_left(hop + 1, o)
                to_core(hop, o)

    hop_arrivals(1)

    arrived("x_right", xg.at[at_zh(-1)])
    part = xg.at[at_zh(-1), pl.ds(0, 4)]
    send("x_far0", part, part, dev(hh=at_zh(1)))
    arrived("x_left", xg.at[at_zh(1)])
    part = xg.at[at_zh(1), pl.ds(4, 4)]
    send("x_far1", part, part, dev(hh=at_zh(-1)))
    arrived("w_far0", wb.at[at_x(2), pl.ds(0, 128)])
    arrived("w_far1", wb.at[at_x(2), pl.ds(128, 128)])
    normed_grad_terms(0)

    hop_arrivals(2)
    normed_grad_terms(-1)
    normed_grad_terms(1)
    normed_grad_sum(0)

    arrived("x_far0", xg.at[at_zh(2), pl.ds(0, 4)])
    arrived("x_far1", xg.at[at_zh(2), pl.ds(4, 4)])

    def turn(yy, carry):
        tiles = [[xg[h, yy, z].astype(F32) for z in range(NZL)] for h in range(NZH)]
        order = [tiles[h][z][8 * c:8 * c + 8] for c in range(NK) for z in range(NZL) for h in range(NZH)]
        xt[:, pl.ds(pl.multiple_of(yy * 128, 128), 128)] = jnp.concatenate(order, axis=0).T.astype(BF16)
        return carry

    lax.fori_loop(0, NY, turn, 0)

    hop_arrivals(3)
    normed_grad_terms(-2)
    normed_grad_terms(2)
    normed_grad_sum(-1)
    normed_grad_sum(1)
    hop_arrivals(4)
    normed_grad_terms(-3)
    normed_grad_terms(3)
    normed_grad_sum(-2)
    normed_grad_sum(2)
    normed_grad_terms(4)

    def weight_grad(xx):
        g = gb[:, :, :, xx].reshape(1024, 384)
        return jnp.dot(xt[...], g, preferred_element_type=F32)

    x1, x2, x3 = at_x(1), at_x(2), at_x(3)
    gwp[x2] = weight_grad(x2).astype(BF16)
    send("gw_a", gwp.at[x2, pl.ds(0, 128)], gw1.at[0], dev(xx=x1))
    send("gw_b", gwp.at[x2, pl.ds(128, 128)], gw1.at[1], dev(xx=x3))
    gwp[x1] = weight_grad(x1).astype(BF16)
    send("gw_c", gwp.at[x1, pl.ds(128, 128)], gw2.at[0, 1], dev(xx=x1))
    gwp[x3] = weight_grad(x3).astype(BF16)
    send("gw_d", gwp.at[x3, pl.ds(0, 128)], gw2.at[1, 0], dev(xx=x3))
    normed_grad_sum(-3)
    normed_grad_sum(3)
    normed_grad_sum(4)
    arrived("gw_a", gw1.at[0])
    gws[0] = (gwp[x1, 0:128].astype(F32) + gw1[0].astype(F32)).astype(BF16)
    send("gw_e", gws.at[0], gw2.at[0, 0], dev(xx=x1))
    arrived("gw_b", gw1.at[1])
    gws[1] = (gwp[x3, 128:256].astype(F32) + gw1[1].astype(F32)).astype(BF16)
    send("gw_f", gws.at[1], gw2.at[1, 1], dev(xx=x3))
    gw_own[...] = weight_grad(x)

    for s, o in far:
        arrived(("f", s, o), fr.at[at_y(-s), zls[o]])
    for b in range(NY * NZL):
        tile = fr[b // NZL, b % NZL].astype(F32)
        fk_keep[b] = jnp.where(k == 0, tile[:8], tile[8:])
        fk_send[b] = jnp.where(k == 0, tile[8:], tile[:8])
    send("fk", fk_send, fk_recv, core_peer)
    arrived("fk", fk_recv)
    rows = x_ref[...].astype(F32)
    inv = lax.rsqrt(jnp.mean(rows * rows, axis=-1, keepdims=True) + 1e-06)
    dot = jnp.zeros((8, 256), F32)
    blocks = []
    for b in range(NY * NZL):
        keep, recv = fk_keep[b], fk_recv[b]
        for j, part in enumerate([jnp.where(k == 0, keep, recv), jnp.where(k == 0, recv, keep)]):
            cols = slice((2 * b + j) * 256, (2 * b + j + 1) * 256)
            dot += (part * gain_ref[:, cols]) * (rows[:, cols] * inv)
            blocks.append((part, cols))
    mean = jnp.sum(dot, axis=-1, keepdims=True) * (1.0 / (256 * len(blocks)))
    for part, cols in blocks:
        dx_ref[:, cols] = (inv * (part * gain_ref[:, cols] - rows[:, cols] * inv * mean)).astype(BF16)

    arrived("gw_c", gw2.at[0, 1])
    arrived("gw_d", gw2.at[1, 0])
    arrived("gw_e", gw2.at[0, 0])
    arrived("gw_f", gw2.at[1, 1])
    for half in (0, 1):
        at = slice(128 * half, 128 * half + 128)
        total = gw_own[at] + gw2[0, half].astype(F32) + gw2[1, half].astype(F32)
        gkv_ref[at] = total[:, :128]
        gq_ref[at] = total[:, 128:]
    for src, slot in pending:
        pltpu.make_async_copy(src, src, send_sems.at[slot]).wait()
    assert len(names) == N_COPIES, len(names)


def on_device(block_input, norm_scale_weight, kv_weight, q_weight, kv_cotangent, q_cotangent):
    vmem = pl.BlockSpec(memory_space=pltpu.VMEM)

    def buf(dtype, *shape):
        return pltpu.VMEM(shape, dtype)

    return pl.pallas_call(
        kernel,
        out_shape=(
            jax.ShapeDtypeStruct((8, 8192), BF16),
            jax.ShapeDtypeStruct((256, 128), F32),
            jax.ShapeDtypeStruct((256, 256), F32),
        ),
        in_specs=[vmem] * 6,
        out_specs=(vmem,) * 3,
        scratch_shapes=[
            buf(F32, 16, 8, 256), buf(F32, 16, 8, 256), buf(F32, 16, 8, 256),
            buf(BF16, 16, 16, 256), buf(BF16, 4, 8, 2, 16, 256), buf(BF16, 256, 1024),
            buf(BF16, 4, 256, 384), buf(BF16, 128, 128), buf(BF16, 128, 128),
            buf(BF16, 4, 32, 384), buf(BF16, 8, 2, 2, 4, 32, 384),
            buf(BF16, 8, 4, 2, 16, 256), buf(BF16, 8, 4, 2, 16, 256),
            buf(BF16, 8, 2, 16, 256), buf(BF16, 8, 2, 16, 256),
            buf(F32, 16, 8, 256), buf(F32, 16, 8, 256), buf(F32, 16, 8, 256),
            buf(BF16, 4, 256, 384), buf(F32, 256, 384), buf(BF16, 2, 128, 384),
            buf(BF16, 2, 2, 128, 384), buf(BF16, 2, 128, 384),
            pltpu.SemaphoreType.DMA((N_COPIES,)), pltpu.SemaphoreType.DMA((N_COPIES,)),
        ],
        compiler_params=pltpu.CompilerParams(
            collective_id=0, has_side_effects=True, vmem_limit_bytes=40 * 1024 * 1024
        ),
        cost_estimate=pl.CostEstimate(flops=1_700_000_000, bytes_accessed=2_000_000, transcendentals=16),
        name="qkv_backward",
    )(
        block_input, norm_scale_weight.reshape(1, -1), kv_weight, q_weight,
        kv_cotangent.reshape(kv_cotangent.shape[0], -1), q_cotangent,
    )


def solution(mesh):
    in_specs = (
        P(("context", "tensor"), None),
        P(),
        P("context", "tensor"),
        P("context", "tensor"),
        P("context", "tensor", None),
        P("context", "tensor"),
    )
    out_specs = (P(("context", "tensor"), None), P("context", "tensor"), P("context", "tensor"))
    return jax.shard_map(
        on_device, mesh=mesh, in_specs=in_specs, out_specs=out_specs, check_vma=False
    )
```

```python
import jax
import jax.numpy as jnp
from jax import lax
from jax.experimental import pallas as pl
from jax.experimental.pallas import tpu as pltpu
from jax.sharding import PartitionSpec as P

NY, NZL, NK = 8, 2, 2
NX, NZH = 4, 4
F32, BF16 = jnp.float32, jnp.bfloat16
N_SEND, N_RECV = 29, 153
VL = 63_400_000


def kernel(
    x_hbm, gain_hbm, kvw_hbm, qw_hbm, kvc_hbm, qc_hbm,
    dx_ref, gkv_ref, gq_ref,
    x_ref, gain_ref, kvw_ref, qw_ref, kvc_ref, qc_ref, unit_ref,
    xk_keep, xk_send, xk_recv, xb, xg, xt,
    wb, ks, kb, gs, gb,
    pb, pr, fb, fr, fk_keep, fk_send, fk_recv,
    gwp, gw_own, gw1, gw2, gws,
    load_sems, send_sems, recv_sems,
):
    loads = [
        pltpu.make_async_copy(src, dst, load_sems.at[i])
        for i, (src, dst) in enumerate([
            (x_hbm, x_ref), (gain_hbm, gain_ref), (kvc_hbm, kvc_ref),
            (qc_hbm, qc_ref), (kvw_hbm, kvw_ref), (qw_hbm, qw_ref),
        ])
    ]
    for load in loads:
        load.start()

    context = lax.axis_index("context")
    tensor = lax.axis_index("tensor")
    y, zl, k = lax.div(context, NZL * NK), lax.rem(lax.div(context, NK), NZL), lax.rem(context, NK)
    x, zh = lax.div(tensor, NZH), lax.rem(tensor, NZH)
    ozl, ok = 1 - zl, 1 - k
    parity = lax.rem(zh, 2)
    ozh = zh + 1 - 2 * parity

    def at_y(step):
        return lax.rem(y + (step + NY) % NY, NY)

    def at_x(step):
        return lax.rem(x + (step + NX) % NX, NX)

    def at_zh(step):
        return lax.rem(zh + (step + NZH) % NZH, NZH)

    def dev(yy=y, zz=zl, kk=k, xx=x, hh=zh):
        return {"context": (yy * NZL + zz) * NK + kk, "tensor": xx * NZH + hh}

    zls = (zl, ozl)
    far = [(s, o) for s in range(NY) for o in range(2) if (s, o) != (0, 0)]
    core_peer = dev(kk=ok)
    right, left = dev(yy=at_y(1)), dev(yy=at_y(-1))

    recv_names, send_names = {}, {}

    def send(name, src, dst, to, group=None):
        slot = recv_names.setdefault(name, len(recv_names))
        group = name if group is None else group
        sent = send_names.setdefault(group, len(send_names))
        pltpu.make_async_remote_copy(
            src_ref=src, dst_ref=dst, send_sem=send_sems.at[sent], recv_sem=recv_sems.at[slot],
            device_id=to, device_id_type=pl.DeviceIdType.MESH,
        ).start()
        pending.setdefault(group, src)

    def arrived(name, dst):
        slot = recv_names.setdefault(name, len(recv_names))
        pltpu.make_async_copy(dst, dst, recv_sems.at[slot]).wait()

    pending = {}

    def drain():
        for group, src in pending.items():
            pltpu.make_async_copy(src, src, send_sems.at[send_names[group]]).wait()
        pending.clear()

    peers = [dev(yy=at_y(s), zz=zls[o]) for s, o in far]
    peers += [dev(hh=at_zh(s)) for s in range(1, NZH)]
    peers += [dev(xx=at_x(s)) for s in range(1, NX)]
    peers += [dev(xx=at_x(s), hh=ozh) for s in range(1, NX)]
    peers += [core_peer]
    barrier = pltpu.get_barrier_semaphore()
    for peer in peers:
        pl.semaphore_signal(barrier, inc=1, device_id=peer, device_id_type=pl.DeviceIdType.MESH)

    loads[2].wait()
    loads[3].wait()
    for j in range(NX):
        part = kvc_ref[32 * j:32 * j + 32, :]
        keys, values = part[:, :128], part[:, 128:]
        gs[j, :, :128] = jnp.where(parity == 0, keys, values)
        gs[j, :, 128:] = qc_ref[32 * j:32 * j + 32, :]
        ks[j] = jnp.where(parity == 0, values, keys)
    pl.semaphore_wait(barrier, len(peers))
    send(("kb", 0), ks.at[x], kb.at[x], dev(hh=ozh))
    for s in (2, 1, 3):
        send(("kb", s), ks.at[at_x(s)], kb.at[x], dev(xx=at_x(s), hh=ozh))
        send(("ga", s), gs.at[at_x(s)], gb.at[y, k, zl, x], dev(xx=at_x(s)))
    gb[y, k, zl, x] = gs[x]

    loads[0].wait()
    loads[1].wait()
    rows = x_ref[...].astype(F32)
    inv = lax.rsqrt(jnp.mean(rows * rows, axis=-1, keepdims=True) + 1e-06)
    for b in range(NY * NZL):
        both = []
        for j in (0, 1):
            cols = slice((2 * b + j) * 256, (2 * b + j + 1) * 256)
            unit = rows[:, cols] * inv
            unit_ref[:, cols] = unit
            both.append((unit * gain_ref[:, cols]).astype(BF16).astype(F32))
        xk_keep[b] = jnp.where(k == 0, both[0], both[1])
        xk_send[b] = jnp.where(k == 0, both[1], both[0])
    send("xk", xk_send, xk_recv, core_peer)

    loads[4].wait()
    loads[5].wait()
    wb[x, :, :128] = kvw_ref[...]
    wb[x, :, 128:] = qw_ref[...]
    send("w_right", wb.at[x], wb.at[x], dev(xx=at_x(1)))
    send("w_left", wb.at[x], wb.at[x], dev(xx=at_x(-1)))

    arrived("xk", xk_recv)
    for b in range(NY * NZL):
        keep, recv = xk_keep[b], xk_recv[b]
        pair = [jnp.where(k == 0, keep, recv), jnp.where(k == 0, recv, keep)]
        xb[b] = jnp.concatenate(pair, axis=0).astype(BF16)
    for s, o in far:
        send(("xa", s, o), xb.at[at_y(s) * NZL + zls[o]], xg.at[zh, y, zl], dev(yy=at_y(s), zz=zls[o]), "xa")
    pending["xa"] = xb.at[pl.ds(0, 15)]
    xg[zh, y, zl] = xb[y * NZL + zl]

    def block(step, o):
        return gb.at[at_y(step), k, zls[o]]

    def ring(hop, o, s):
        piece = at_x(-s)
        if hop < 4 or (hop == 4 and o == 0):
            at = block(1 - hop, o).at[piece]
            send(("gr", hop, o, s), at, at, right, "ring")
        if hop < 4 or (hop == 4 and o == 1):
            at = block(hop - 1, o).at[piece]
            send(("gl", hop, o, s), at, at, left, "ring")

    def to_core(step, o):
        send(("gk", step, o), block(step, o), block(step, o), core_peer, "gk")

    pieces = (0, 1, 3, 2)
    for s in pieces:
        piece = at_x(-s)
        arrived(("kb", s), kb.at[piece])
        if s:
            arrived(("ga", s), gb.at[y, k, zl, piece])
        head = gb[y, k, zl, piece, :, :128].astype(F32) + kb[piece].astype(F32)
        gb[y, k, zl, piece, :, :128] = head.astype(BF16)
        ring(1, 0, s)
        at = block(0, 0).at[piece]
        send(("gz", s), at, at, dev(zz=ozl), "gz")
    pending["gz"] = block(0, 0)
    to_core(0, 0)

    def hop_arrivals(hop, o):
        if hop == 0:
            for s in pieces:
                arrived(("gz", s), block(0, 1).at[at_x(-s)])
                ring(1, 1, s)
            to_core(0, 1)
            return
        for s in pieces:
            if hop < 4 or o == 0:
                arrived(("gr", hop, o, s), block(-hop, o).at[at_x(-s)])
            if hop < 4 or o == 1:
                arrived(("gl", hop, o, s), block(hop, o).at[at_x(-s)])
            ring(hop + 1, o, s)
        if hop < 4:
            to_core(-hop, o)
        to_core(hop, o)

    def normed_grad_terms(step):
        yy = at_y(step)
        for o in (0, 1):
            arrived(("gk", step, o), gb.at[yy, ok, zls[o]])
        acc = jnp.zeros((128, 256), F32)
        for j in range(NX):
            acc += lax.dot_general(
                gb[yy, :, :, j].reshape(128, 384), wb[j], (((1,), (1,)), ((), ())), preferred_element_type=F32
            )
        for h in range(NZH):
            for z in range(NZL):
                start = z * 32 + h * 8
                pb[yy, h, z] = jnp.concatenate([acc[start:start + 8], acc[64 + start:72 + start]], axis=0).astype(BF16)
        for s in (2, 1, 3):
            send(("p", step, s), pb.at[yy, at_zh(s)], pr.at[yy, zh], dev(hh=at_zh(s)), "p")

    def normed_grad_sum(step):
        yy = at_y(step)
        for s in (1, 3, 2):
            arrived(("p", step, s), pr.at[yy, at_zh(-s)])
        total = pb[yy, zh].astype(F32)
        for s in (1, 2, 3):
            total += pr[yy, at_zh(s)].astype(F32)
        fb[yy] = total.astype(BF16)
        for o in (0, 1):
            if (step, o) != (0, 0):
                send(("f", step % NY, o), fb.at[yy, zls[o]], fr.at[y, zl], dev(yy=yy, zz=zls[o]), "f")
        if step == 0:
            fr[y, zl] = fb[y, zl]

    hop_arrivals(1, 0)
    hop_arrivals(0, 1)

    for s, o in far:
        arrived(("xa", s, o), xg.at[zh, at_y(-s), zls[o]])
    send("x_right", xg.at[zh], xg.at[zh], dev(hh=at_zh(1)))
    send("x_left", xg.at[zh], xg.at[zh], dev(hh=at_zh(-1)))

    arrived("w_right", wb.at[at_x(-1)])
    part = wb.at[at_x(-1), pl.ds(0, 128)]
    send("w_far0", part, part, dev(xx=at_x(1)))
    arrived("w_left", wb.at[at_x(1)])
    part = wb.at[at_x(1), pl.ds(128, 128)]
    send("w_far1", part, part, dev(xx=at_x(-1)))

    hop_arrivals(2, 0)
    hop_arrivals(1, 1)

    arrived("x_right", xg.at[at_zh(-1)])
    part = xg.at[at_zh(-1), pl.ds(0, 4)]
    send("x_far0", part, part, dev(hh=at_zh(1)))
    arrived("x_left", xg.at[at_zh(1)])
    part = xg.at[at_zh(1), pl.ds(4, 4)]
    send("x_far1", part, part, dev(hh=at_zh(-1)))
    arrived("w_far0", wb.at[at_x(2), pl.ds(0, 128)])
    arrived("w_far1", wb.at[at_x(2), pl.ds(128, 128)])
    normed_grad_terms(0)

    hop_arrivals(3, 0)
    normed_grad_terms(-1)
    normed_grad_terms(1)
    hop_arrivals(2, 1)
    hop_arrivals(4, 0)
    normed_grad_terms(-2)
    normed_grad_terms(2)
    hop_arrivals(3, 1)

    arrived("x_far0", xg.at[at_zh(2), pl.ds(0, 4)])
    arrived("x_far1", xg.at[at_zh(2), pl.ds(4, 4)])

    def turn(yy, carry):
        tiles = [[xg[h, yy, z].astype(F32) for z in range(NZL)] for h in range(NZH)]
        order = [tiles[h][z][8 * c:8 * c + 8] for c in range(NK) for z in range(NZL) for h in range(NZH)]
        xt[:, pl.ds(pl.multiple_of(yy * 128, 128), 128)] = jnp.concatenate(order, axis=0).T.astype(BF16)
        return carry

    lax.fori_loop(0, NY, turn, 0)

    hop_arrivals(4, 1)
    pending["ring"], pending["gk"] = gb.at[pl.ds(0, 7), 0], gb.at[:, 0]
    normed_grad_terms(-3)
    normed_grad_terms(3)
    normed_grad_terms(4)
    pending["p"] = pb.at[:, pl.ds(0, 3)]

    def weight_grad(xx):
        g = gb[:, :, :, xx].reshape(1024, 384)
        return jnp.dot(xt[...], g, preferred_element_type=F32)

    x1, x2, x3 = at_x(1), at_x(2), at_x(3)
    gwp[x2] = weight_grad(x2).astype(BF16)
    send("gw_a", gwp.at[x2, pl.ds(0, 128)], gw1.at[0], dev(xx=x1))
    send("gw_b", gwp.at[x2, pl.ds(128, 128)], gw1.at[1], dev(xx=x3))
    for step in (0, -1, 1, -2, 2):
        normed_grad_sum(step)
    gwp[x1] = weight_grad(x1).astype(BF16)
    send("gw_c", gwp.at[x1, pl.ds(128, 128)], gw2.at[0, 1], dev(xx=x1))
    gwp[x3] = weight_grad(x3).astype(BF16)
    send("gw_d", gwp.at[x3, pl.ds(0, 128)], gw2.at[1, 0], dev(xx=x3))
    normed_grad_sum(-3)
    normed_grad_sum(3)
    normed_grad_sum(4)
    pending["f"] = xb.at[pl.ds(0, 15)]
    gw_own[...] = weight_grad(x)
    arrived("gw_a", gw1.at[0])
    gws[0] = (gwp[x1, 0:128].astype(F32) + gw1[0].astype(F32)).astype(BF16)
    send("gw_e", gws.at[0], gw2.at[0, 0], dev(xx=x1))
    arrived("gw_b", gw1.at[1])
    gws[1] = (gwp[x3, 128:256].astype(F32) + gw1[1].astype(F32)).astype(BF16)
    send("gw_f", gws.at[1], gw2.at[1, 1], dev(xx=x3))
    drain()
    arrived("gw_c", gw2.at[0, 1])
    arrived("gw_d", gw2.at[1, 0])
    arrived("gw_e", gw2.at[0, 0])
    arrived("gw_f", gw2.at[1, 1])
    for half in (0, 1):
        at = slice(128 * half, 128 * half + 128)
        total = gw_own[at] + gw2[0, half].astype(F32) + gw2[1, half].astype(F32)
        gkv_ref[at] = total[:, :128]
        gq_ref[at] = total[:, 128:]

    for s, o in far:
        arrived(("f", s, o), fr.at[at_y(-s), zls[o]])
    for b in range(NY * NZL):
        tile = fr[b // NZL, b % NZL].astype(F32)
        fk_keep[b] = jnp.where(k == 0, tile[:8], tile[8:])
        fk_send[b] = jnp.where(k == 0, tile[8:], tile[:8])
    send("fk", fk_send, fk_recv, core_peer)
    arrived("fk", fk_recv)
    dot = jnp.zeros((8, 256), F32)
    blocks = []
    for b in range(NY * NZL):
        keep, recv = fk_keep[b], fk_recv[b]
        for j, part in enumerate([jnp.where(k == 0, keep, recv), jnp.where(k == 0, recv, keep)]):
            cols = slice((2 * b + j) * 256, (2 * b + j + 1) * 256)
            scaled = part * gain_ref[:, cols]
            dot += scaled * unit_ref[:, cols]
            blocks.append((scaled, cols))
    mean = jnp.sum(dot, axis=-1, keepdims=True) * (1.0 / (256 * len(blocks)))
    for scaled, cols in blocks:
        dx_ref[:, cols] = (inv * (scaled - unit_ref[:, cols] * mean)).astype(BF16)
    drain()
    assert (len(send_names), len(recv_names)) == (N_SEND, N_RECV), (len(send_names), len(recv_names))


def on_device(block_input, norm_scale_weight, kv_weight, q_weight, kv_cotangent, q_cotangent):
    vmem = pl.BlockSpec(memory_space=pltpu.VMEM)
    hbm = pl.BlockSpec(memory_space=pltpu.HBM)

    def buf(dtype, *shape):
        return pltpu.VMEM(shape, dtype)

    return pl.pallas_call(
        kernel,
        out_shape=(
            jax.ShapeDtypeStruct((8, 8192), BF16),
            jax.ShapeDtypeStruct((256, 128), F32),
            jax.ShapeDtypeStruct((256, 256), F32),
        ),
        in_specs=[hbm] * 6,
        out_specs=(vmem,) * 3,
        scratch_shapes=[
            buf(BF16, 8, 8192), buf(F32, 1, 8192), buf(BF16, 256, 128), buf(BF16, 256, 256),
            buf(BF16, 128, 256), buf(BF16, 128, 256), buf(F32, 8, 8192),
            buf(F32, 16, 8, 256), buf(F32, 16, 8, 256), buf(F32, 16, 8, 256),
            buf(BF16, 16, 16, 256), buf(BF16, 4, 8, 2, 16, 256), buf(BF16, 256, 1024),
            buf(BF16, 4, 256, 384), buf(BF16, 4, 32, 128), buf(BF16, 4, 32, 128),
            buf(BF16, 4, 32, 384), buf(BF16, 8, 2, 2, 4, 32, 384),
            buf(BF16, 8, 4, 2, 16, 256), buf(BF16, 8, 4, 2, 16, 256),
            buf(BF16, 8, 2, 16, 256), buf(BF16, 8, 2, 16, 256),
            buf(F32, 16, 8, 256), buf(F32, 16, 8, 256), buf(F32, 16, 8, 256),
            buf(BF16, 4, 256, 384), buf(F32, 256, 384), buf(BF16, 2, 128, 384),
            buf(BF16, 2, 2, 128, 384), buf(BF16, 2, 128, 384),
            pltpu.SemaphoreType.DMA((6,)),
            pltpu.SemaphoreType.DMA((N_SEND,)), pltpu.SemaphoreType.DMA((N_RECV,)),
        ],
        compiler_params=pltpu.CompilerParams(
            collective_id=0, has_side_effects=True, vmem_limit_bytes=VL
        ),
        cost_estimate=pl.CostEstimate(flops=1_700_000_000, bytes_accessed=2_000_000, transcendentals=16),
        name="qkv_backward",
    )(
        block_input, norm_scale_weight.reshape(1, -1), kv_weight, q_weight,
        kv_cotangent.reshape(kv_cotangent.shape[0], -1), q_cotangent,
    )


def solution(mesh):
    in_specs = (
        P(("context", "tensor"), None),
        P(),
        P("context", "tensor"),
        P("context", "tensor"),
        P("context", "tensor", None),
        P("context", "tensor"),
    )
    out_specs = (P(("context", "tensor"), None), P("context", "tensor"), P("context", "tensor"))
    return jax.shard_map(
        on_device, mesh=mesh, in_specs=in_specs, out_specs=out_specs, check_vma=False
    )
```

```python
import jax
import jax.numpy as jnp
from jax import lax
from jax.experimental import pallas as pl
from jax.experimental.pallas import tpu as pltpu
from jax.sharding import PartitionSpec as P

NY, NZL, NK = 8, 2, 2
NX, NZH = 4, 4
F32, BF16 = jnp.float32, jnp.bfloat16
N_SEND, N_RECV = 46, 196
VL = 63_400_000


def kernel(
    x_hbm, gain_hbm, kvw_hbm, qw_hbm, kvc_hbm, qc_hbm,
    dx_hbm, gkv_hbm, gq_hbm,
    dx_ref, gkv_ref, gq_ref,
    x_ref, gain_ref, kvw_ref, qw_ref, kvc_ref, qc_ref, unit_ref, scaled_ref,
    xk_keep, xk_send, xk_recv, xb, xg, xt,
    wb, va, ka, ks, kb, gq, gv,
    pb, pr, fb, fr, fk_keep, fk_send, fk_recv,
    gwp, gw_own, gw1, gw2, gws,
    load_sems, store_sems, send_sems, recv_sems,
):
    loads = [
        pltpu.make_async_copy(src, dst, load_sems.at[i])
        for i, (src, dst) in enumerate([
            (x_hbm, x_ref), (gain_hbm, gain_ref), (qc_hbm, qc_ref),
            (kvc_hbm, kvc_ref), (kvw_hbm, kvw_ref), (qw_hbm, qw_ref),
        ])
    ]
    for load in loads:
        load.start()

    context = lax.axis_index("context")
    tensor = lax.axis_index("tensor")
    y, zl, k = lax.div(context, NZL * NK), lax.rem(lax.div(context, NK), NZL), lax.rem(context, NK)
    x, zh = lax.div(tensor, NZH), lax.rem(tensor, NZH)
    ozl, ok = 1 - zl, 1 - k
    parity = lax.rem(zh, 2)
    ozh = zh + 1 - 2 * parity

    def at_y(step):
        return lax.rem(y + (step + NY) % NY, NY)

    def at_x(step):
        return lax.rem(x + (step + NX) % NX, NX)

    def at_zh(step):
        return lax.rem(zh + (step + NZH) % NZH, NZH)

    def dev(yy=y, zz=zl, kk=k, xx=x, hh=zh):
        return {"context": (yy * NZL + zz) * NK + kk, "tensor": xx * NZH + hh}

    zls = (zl, ozl)
    far = [(s, o) for s in range(NY) for o in range(2) if (s, o) != (0, 0)]
    core_peer = dev(kk=ok)
    right, left = dev(yy=at_y(1)), dev(yy=at_y(-1))

    recv_names, send_names = {}, {}

    steps = (0, 1, 7, 2, 6, 3, 5, 4)
    parts = ((0, 3), (3, 5), (5, 8))

    def send(name, src, dst, to, group=None):
        slot = recv_names.setdefault(name, len(recv_names))
        group = name if group is None else group
        sent = send_names.setdefault(group, len(send_names))
        pltpu.make_async_remote_copy(
            src_ref=src, dst_ref=dst, send_sem=send_sems.at[sent], recv_sem=recv_sems.at[slot],
            device_id=to, device_id_type=pl.DeviceIdType.MESH,
        ).start()
        pending.setdefault(group, src)

    def arrived(name, dst):
        slot = recv_names.setdefault(name, len(recv_names))
        pltpu.make_async_copy(dst, dst, recv_sems.at[slot]).wait()

    pending = {}

    def drain():
        for group, src in pending.items():
            pltpu.make_async_copy(src, src, send_sems.at[send_names[group]]).wait()
        pending.clear()

    peers = [dev(yy=at_y(s), zz=zls[o]) for s, o in far]
    peers += [dev(hh=at_zh(s)) for s in range(1, NZH)]
    peers += [dev(xx=at_x(s)) for s in range(1, NX)]
    peers += [dev(xx=at_x(s), hh=ozh) for s in range(1, NX)]
    peers += [core_peer]
    barrier = pltpu.get_barrier_semaphore()
    for peer in peers:
        pl.semaphore_signal(barrier, inc=1, device_id=peer, device_id_type=pl.DeviceIdType.MESH)

    def goes(hop, o, right_way, piece):
        return hop < 4 or (hop == 4 and right_way == ((piece in (0, 1, 2)) == (o == 0)))

    def ring_send(kind, buf, hop, o, at, piece):
        for right_way in (True, False):
            if goes(hop, o, right_way, piece):
                ref = buf.at[at_y(1 - hop if right_way else hop - 1), k, zls[o]].at[at]
                name = (kind + ("r" if right_way else "l"), hop, o, piece)
                send(name, ref, ref, right if right_way else left, kind + "ring" + str(o))

    def ring_q(hop, o, s):
        ring_send("q", gq, hop, o, s, s)

    def ring_v(hop, o):
        ring_send("v", gv, hop, o, pl.ds(0, NX), "v")

    def cross(kind, buf, at, piece):
        ref = buf.at[y, k, zl].at[at]
        send((kind + "z", piece), ref, ref, dev(zz=ozl), kind + "z")

    def start_q(s):
        ring_q(1, 0, s)
        cross("q", gq, s, s)

    def to_core(kind, buf, step, o):
        ref = buf.at[at_y(step), k, zls[o]]
        send((kind + "k", step, o), ref, ref, core_peer, kind + "k")

    loads[2].wait()
    loads[3].wait()
    gq[y, k, zl, 0] = qc_ref[pl.ds(pl.multiple_of(32 * x, 32), 32), :]
    for j in range(NX):
        part = kvc_ref[32 * j:32 * j + 32, :]
        keys, values = part[:, :128], part[:, 128:]
        va[j] = jnp.where(parity == 0, keys, values)
        ks[j] = jnp.where(parity == 0, values, keys)
    pl.semaphore_wait(barrier, len(peers))
    start_q(0)
    for s in (2, 1, 3):
        there = at_x(s)
        send(("qa", s), qc_ref.at[pl.ds(pl.multiple_of(32 * there, 32), 32)], gq.at[y, k, zl, s], dev(xx=there))
    for s in (2, 1, 3):
        send(("kb", s), ks.at[at_x(s)], kb.at[s], dev(xx=at_x(s), hh=ozh))
        send(("ka", s), va.at[at_x(s)], ka.at[s], dev(xx=at_x(s)))
    send(("kb", 0), ks.at[x], kb.at[0], dev(hh=ozh))
    ka[0] = va[x]

    loads[0].wait()
    loads[1].wait()
    rows = x_ref[...].astype(F32)
    inv = lax.rsqrt(jnp.mean(rows * rows, axis=-1, keepdims=True) + 1e-06)
    for b in range(NY * NZL):
        both = []
        for j in (0, 1):
            cols = slice((2 * b + j) * 256, (2 * b + j + 1) * 256)
            unit = rows[:, cols] * inv
            unit_ref[:, cols] = unit
            both.append((unit * gain_ref[:, cols]).astype(BF16).astype(F32))
        xk_keep[b] = jnp.where(k == 0, both[0], both[1])
        xk_send[b] = jnp.where(k == 0, both[1], both[0])
    send("xk", xk_send, xk_recv, core_peer)

    loads[4].wait()
    loads[5].wait()
    wb[0, :, :128] = kvw_ref[...]
    wb[0, :, 128:] = qw_ref[...]
    send("w_right", wb.at[0], wb.at[1], dev(xx=at_x(1)))
    send("w_left", wb.at[0], wb.at[3], dev(xx=at_x(-1)))

    arrived("xk", xk_recv)
    for b in range(NY * NZL):
        keep, recv = xk_keep[b], xk_recv[b]
        pair = [jnp.where(k == 0, keep, recv), jnp.where(k == 0, recv, keep)]
        xb[b] = jnp.concatenate(pair, axis=0).astype(BF16)
    for s, o in far:
        there = steps.index((-s) % NY)
        send(("xa", s, o), xb.at[at_y(s) * NZL + zls[o]], xg.at[zh, there, zl], dev(yy=at_y(s), zz=zls[o]), "xa")
    pending["xa"] = xb.at[pl.ds(0, 15)]
    xg[zh, 0, zl] = xb[y * NZL + zl]

    for s in (1, 3, 2):
        arrived(("qa", s), gq.at[y, k, zl, s])
        start_q(s)
    to_core("q", gq, 0, 0)

    def pass_on(kind, buf, hop, o, at, piece):
        steps = [step for step in ((-hop, hop) if hop < 4 else (4,))]
        for step in steps:
            right_way = goes(hop, o, True, piece) if hop == 4 else step < 0
            arrived((kind + ("r" if right_way else "l"), hop, o, piece), buf.at[at_y(step), k, zls[o]].at[at])
        ring_send(kind, buf, hop + 1, o, at, piece)

    def rows_part(p):
        first, last = parts[p]
        for n in range(first, last):
            for o in (0, 1):
                if (n, o) != (0, 0):
                    arrived(("xa", (-steps[n]) % NY, o), xg.at[zh, n, zls[o]])
        at = xg.at[zh, pl.ds(first, last - first)]
        send(("x_right", p), at, at, dev(hh=at_zh(1)))
        send(("x_left", p), at, at, dev(hh=at_zh(-1)))

    def rows_far(p):
        first, last = parts[p]
        for name, step, z, to in (("x_right", -1, 0, 1), ("x_left", 1, 1, -1)):
            arrived((name, p), xg.at[at_zh(step), pl.ds(first, last - first)])
            at = xg.at[at_zh(step), pl.ds(first, last - first), z]
            send((name, p, "far"), at, at, dev(hh=at_zh(to)))

    def hop_core(kind, buf, hop, o):
        if 0 < hop < 4:
            to_core(kind, buf, -hop, o)
        to_core(kind, buf, hop, o)

    def hop_q(hop, o):
        for s in (0, 1, 3, 2):
            pass_on("q", gq, hop, o, s, s)
        hop_core("q", gq, hop, o)

    def hop_v(hop, o):
        pass_on("v", gv, hop, o, pl.ds(0, NX), "v")
        hop_core("v", gv, hop, o)

    def crossed_q():
        for s in (0, 1, 3, 2):
            arrived(("qz", s), gq.at[y, k, ozl, s])
            ring_q(1, 1, s)
        to_core("q", gq, 0, 1)

    def crossed_v():
        arrived(("vz", "v"), gv.at[y, k, ozl])
        ring_v(1, 1)
        to_core("v", gv, 0, 1)

    def pair_heads():
        for s in range(NX):
            if s:
                arrived(("ka", s), ka.at[s])
            arrived(("kb", s), kb.at[s])
        gv[y, k, zl] = (ka[...].astype(F32) + kb[...].astype(F32)).astype(BF16)
        ring_v(1, 0)
        cross("v", gv, pl.ds(0, NX), "v")
        to_core("v", gv, 0, 0)

    def normed_grad_terms(step):
        yy = at_y(step)
        for o in (0, 1):
            arrived(("qk", step, o), gq.at[yy, ok, zls[o]])
            arrived(("vk", step, o), gv.at[yy, ok, zls[o]])
        acc = jnp.zeros((128, 256), F32)
        for j in range(NX):
            acc += lax.dot_general(
                gq[yy, :, :, j].reshape(128, 256), wb[j, :, 128:], (((1,), (1,)), ((), ())), preferred_element_type=F32
            )
            acc += lax.dot_general(
                gv[yy, :, :, j].reshape(128, 128), wb[j, :, :128], (((1,), (1,)), ((), ())), preferred_element_type=F32
            )
        for h in range(NZH):
            for z in range(NZL):
                start = z * 32 + h * 8
                pb[yy, h, z] = jnp.concatenate([acc[start:start + 8], acc[64 + start:72 + start]], axis=0).astype(BF16)
        for s in (2, 1, 3):
            send(("p", step, s), pb.at[yy, at_zh(s)], pr.at[yy, zh], dev(hh=at_zh(s)), "p")

    def normed_grad_sum(step):
        yy = at_y(step)
        for s in (1, 3, 2):
            arrived(("p", step, s), pr.at[yy, at_zh(-s)])
        total = pb[yy, zh].astype(F32)
        for s in (1, 2, 3):
            total += pr[yy, at_zh(s)].astype(F32)
        fb[yy] = total.astype(BF16)
        for o in (0, 1):
            if (step, o) != (0, 0):
                send(("f", step % NY, o), fb.at[yy, zls[o]], fr.at[y, zl], dev(yy=yy, zz=zls[o]), "f")
        if step == 0:
            fr[y, zl] = fb[y, zl]

    pair_heads()
    rows_part(0)
    hop_q(1, 0)
    crossed_q()

    arrived("w_right", wb.at[1])
    send("w_far0", wb.at[1, pl.ds(0, 128)], wb.at[2, pl.ds(0, 128)], dev(xx=at_x(1)))
    arrived("w_left", wb.at[3])
    send("w_far1", wb.at[3, pl.ds(128, 128)], wb.at[2, pl.ds(128, 128)], dev(xx=at_x(-1)))

    rows_part(1)
    hop_v(1, 0)
    crossed_v()
    rows_part(2)
    rows_far(0)
    hop_q(2, 0)
    hop_q(1, 1)
    hop_v(2, 0)
    hop_v(1, 1)
    rows_far(1)

    arrived("w_far0", wb.at[2, pl.ds(0, 128)])
    arrived("w_far1", wb.at[2, pl.ds(128, 128)])
    normed_grad_terms(0)
    hop_q(3, 0)
    rows_far(2)
    normed_grad_terms(-1)
    hop_q(2, 1)
    normed_grad_terms(1)
    hop_v(3, 0)
    hop_v(2, 1)
    hop_q(4, 0)
    hop_q(3, 1)
    hop_v(4, 0)
    normed_grad_terms(-2)
    hop_v(3, 1)
    normed_grad_terms(2)
    hop_q(4, 1)

    normed_grad_terms(-3)
    normed_grad_terms(3)
    hop_v(4, 1)
    pending["qk"], pending["vk"] = gq.at[:, 0], gv.at[:, 0]
    pending["qz"], pending["vz"] = gq.at[0, 0, 0], gv.at[0, 0, 0]
    pending["qring0"], pending["vring0"] = gq.at[pl.ds(0, 7), 0, 0], gv.at[pl.ds(0, 7), 0, 0]
    pending["qring1"], pending["vring1"] = gq.at[pl.ds(0, 7), 0, 0], gv.at[pl.ds(0, 7), 0, 0]
    normed_grad_terms(4)
    pending["p"] = pb.at[:, pl.ds(0, 3)]

    for p, (first, last) in enumerate(parts):
        for name, z in (("x_right", 0), ("x_left", 1)):
            arrived((name, p, "far"), xg.at[at_zh(2), pl.ds(first, last - first), z])

    def turn(n, yy):
        tiles = [[xg[h, n, z].astype(F32) for z in range(NZL)] for h in range(NZH)]
        order = [tiles[h][z][8 * c:8 * c + 8] for c in range(NK) for z in range(NZL) for h in range(NZH)]
        xt[:, pl.ds(pl.multiple_of(yy * 128, 128), 128)] = jnp.concatenate(order, axis=0).T.astype(BF16)

    for n, step in enumerate(steps):
        turn(n, at_y(step))

    def weight_grad(slot, out):
        value = jnp.dot(xt[...], gv[:, :, :, slot].reshape(1024, 128), preferred_element_type=F32)
        out[:, :128] = value.astype(out.dtype)
        query = jnp.dot(xt[...], gq[:, :, :, slot].reshape(1024, 256), preferred_element_type=F32)
        out[:, 128:] = query.astype(out.dtype)

    x1, x3 = at_x(1), at_x(-1)
    weight_grad(2, gwp.at[2])
    send("gw_a", gwp.at[2, pl.ds(0, 128)], gw1.at[0], dev(xx=x1))
    send("gw_b", gwp.at[2, pl.ds(128, 128)], gw1.at[1], dev(xx=x3))
    weight_grad(3, gwp.at[3])
    send("gw_c", gwp.at[3, pl.ds(128, 128)], gw2.at[0, 1], dev(xx=x1))
    weight_grad(1, gwp.at[1])
    send("gw_d", gwp.at[1, pl.ds(0, 128)], gw2.at[1, 0], dev(xx=x3))
    for step in (0, -1, 1, -2, 2):
        normed_grad_sum(step)
    normed_grad_sum(-3)
    normed_grad_sum(3)
    normed_grad_sum(4)
    pending["f"] = xb.at[pl.ds(0, 15)]
    arrived("gw_a", gw1.at[0])
    gws[0] = (gwp[3, 0:128].astype(F32) + gw1[0].astype(F32)).astype(BF16)
    send("gw_e", gws.at[0], gw2.at[0, 0], dev(xx=x1))
    arrived("gw_b", gw1.at[1])
    gws[1] = (gwp[1, 128:256].astype(F32) + gw1[1].astype(F32)).astype(BF16)
    send("gw_f", gws.at[1], gw2.at[1, 1], dev(xx=x3))
    weight_grad(0, gw_own)

    order = [(s, o) for s in steps for o in (0, 1)]
    groups = ((0, 10), (10, 16))

    def swap_cores(g):
        first, last = groups[g]
        for n in range(first, last):
            s, o = order[n]
            at = fr.at[at_y(-s), zls[o]]
            if (s, o) != (0, 0):
                arrived(("f", s, o), at)
            tile = at[...].astype(F32)
            fk_keep[n] = jnp.where(k == 0, tile[:8], tile[8:])
            fk_send[n] = jnp.where(k == 0, tile[8:], tile[:8])
        part = pl.ds(first, last - first)
        send(("fk", g), fk_send.at[part], fk_recv.at[part], core_peer)

    late = {name: pending.pop(name) for name in ("gw_e", "gw_f")}
    drain()
    pending.update(late)
    swap_cores(0)
    arrived("gw_c", gw2.at[0, 1])
    arrived("gw_d", gw2.at[1, 0])
    arrived("gw_e", gw2.at[0, 0])
    arrived("gw_f", gw2.at[1, 1])
    for half in (0, 1):
        at = slice(128 * half, 128 * half + 128)
        total = gw_own[at] + gw2[0, half].astype(F32) + gw2[1, half].astype(F32)
        gkv_ref[at] = total[:, :128]
        gq_ref[at] = total[:, 128:]
    stores = [
        pltpu.make_async_copy(src, dst, store_sems.at[i])
        for i, (src, dst) in enumerate([(gkv_ref, gkv_hbm), (gq_ref, gq_hbm), (dx_ref, dx_hbm)])
    ]
    stores[0].start()
    stores[1].start()

    swap_cores(1)
    dot = jnp.zeros((8, 512), F32)
    for g, (first, last) in enumerate(groups):
        arrived(("fk", g), fk_recv.at[pl.ds(first, last - first)])
        for n in range(first, last):
            s, o = order[n]
            cols = pl.ds(pl.multiple_of((at_y(-s) * NZL + zls[o]) * 512, 512), 512)
            keep, recv = fk_keep[n], fk_recv[n]
            pair = [jnp.where(k == 0, keep, recv), jnp.where(k == 0, recv, keep)]
            scaled = jnp.concatenate(pair, axis=1) * gain_ref[:, cols]
            scaled_ref[:, cols] = scaled
            dot += scaled * unit_ref[:, cols]
    mean = jnp.sum(dot, axis=-1, keepdims=True) * (1.0 / 8192)
    dx_ref[...] = (inv * (scaled_ref[...] - unit_ref[...] * mean)).astype(BF16)
    stores[2].start()
    drain()
    for store in stores:
        store.wait()
    assert (len(send_names), len(recv_names)) == (N_SEND, N_RECV), (len(send_names), len(recv_names))


def hand_over(*refs):
    for i in range(3):
        refs[3 + i][...] = refs[i][...]


def on_device(block_input, norm_scale_weight, kv_weight, q_weight, kv_cotangent, q_cotangent):
    hbm = pl.BlockSpec(memory_space=pltpu.HBM)
    vmem = pl.BlockSpec(memory_space=pltpu.VMEM)

    def buf(dtype, *shape):
        return pltpu.VMEM(shape, dtype)

    outs = pl.pallas_call(
        kernel,
        out_shape=(
            jax.ShapeDtypeStruct((8, 8192), BF16),
            jax.ShapeDtypeStruct((256, 128), F32),
            jax.ShapeDtypeStruct((256, 256), F32),
        ),
        in_specs=[hbm] * 6,
        out_specs=(hbm,) * 3,
        scratch_shapes=[
            buf(BF16, 8, 8192), buf(F32, 256, 128), buf(F32, 256, 256),
            buf(BF16, 8, 8192), buf(F32, 1, 8192), buf(BF16, 256, 128), buf(BF16, 256, 256),
            buf(BF16, 128, 256), buf(BF16, 128, 256), buf(F32, 8, 8192), buf(F32, 8, 8192),
            buf(F32, 16, 8, 256), buf(F32, 16, 8, 256), buf(F32, 16, 8, 256),
            buf(BF16, 16, 16, 256), buf(BF16, 4, 8, 2, 16, 256), buf(BF16, 256, 1024),
            buf(BF16, 4, 256, 384), buf(BF16, 4, 32, 128), buf(BF16, 4, 32, 128),
            buf(BF16, 4, 32, 128), buf(BF16, 4, 32, 128),
            buf(BF16, 8, 2, 2, 4, 32, 256), buf(BF16, 8, 2, 2, 4, 32, 128),
            buf(BF16, 8, 4, 2, 16, 256), buf(BF16, 8, 4, 2, 16, 256),
            buf(BF16, 8, 2, 16, 256), buf(BF16, 8, 2, 16, 256),
            buf(F32, 16, 8, 256), buf(F32, 16, 8, 256), buf(F32, 16, 8, 256),
            buf(BF16, 4, 256, 384), buf(F32, 256, 384), buf(BF16, 2, 128, 384),
            buf(BF16, 2, 2, 128, 384), buf(BF16, 2, 128, 384),
            pltpu.SemaphoreType.DMA((6,)), pltpu.SemaphoreType.DMA((3,)),
            pltpu.SemaphoreType.DMA((N_SEND,)), pltpu.SemaphoreType.DMA((N_RECV,)),
        ],
        compiler_params=pltpu.CompilerParams(
            collective_id=0, has_side_effects=True, vmem_limit_bytes=VL
        ),
        cost_estimate=pl.CostEstimate(flops=1_700_000_000, bytes_accessed=2_000_000, transcendentals=16),
        name="qkv_backward",
    )(
        block_input, norm_scale_weight.reshape(1, -1), kv_weight, q_weight,
        kv_cotangent.reshape(kv_cotangent.shape[0], -1), q_cotangent,
    )
    return pl.pallas_call(
        hand_over,
        out_shape=tuple(jax.ShapeDtypeStruct(out.shape, out.dtype) for out in outs),
        in_specs=[vmem] * 3,
        out_specs=(vmem,) * 3,
        compiler_params=pltpu.CompilerParams(vmem_limit_bytes=VL),
        name="hand_over",
    )(*outs)


def solution(mesh):
    in_specs = (
        P(("context", "tensor"), None),
        P(),
        P("context", "tensor"),
        P("context", "tensor"),
        P("context", "tensor", None),
        P("context", "tensor"),
    )
    out_specs = (P(("context", "tensor"), None), P("context", "tensor"), P("context", "tensor"))
    return jax.shard_map(
        on_device, mesh=mesh, in_specs=in_specs, out_specs=out_specs, check_vma=False
    )
```

```python
import jax
import jax.numpy as jnp
from jax import lax
from jax.experimental import pallas as pl
from jax.experimental.pallas import tpu as pltpu
from jax.sharding import PartitionSpec as P

NY, NZL, NK = 8, 2, 2
NX, NZH = 4, 4
F32, BF16 = jnp.float32, jnp.bfloat16
N_SEND, N_RECV = 17, 136
VL = 63_400_000


def kernel(
    x_hbm, gain_hbm, kvw_hbm, qw_hbm, kvc_hbm, qc_hbm,
    dn_hbm, own_hbm, gw2,
    x_ref, gain_ref, kvw_ref, qw_ref, kvc_ref, qc_ref,
    xk_keep, xk_send, xk_recv, xb, xg, xt,
    wb, va, ka, ks, kb, gq, gv,
    pb, pr, fb, fr, fk_keep, fk_send,
    gwp, gw_own, gw1, gws,
    load_sems, store_sems, send_sems, recv_sems,
):
    loads = [
        pltpu.make_async_copy(src, dst, load_sems.at[i])
        for i, (src, dst) in enumerate([
            (x_hbm, x_ref), (gain_hbm, gain_ref), (qc_hbm, qc_ref),
            (kvc_hbm, kvc_ref), (kvw_hbm, kvw_ref), (qw_hbm, qw_ref),
        ])
    ]
    for load in loads:
        load.start()

    context = lax.axis_index("context")
    tensor = lax.axis_index("tensor")
    y, zl, k = lax.div(context, NZL * NK), lax.rem(lax.div(context, NK), NZL), lax.rem(context, NK)
    x, zh = lax.div(tensor, NZH), lax.rem(tensor, NZH)
    ozl, ok = 1 - zl, 1 - k
    parity = lax.rem(zh, 2)
    ozh = zh + 1 - 2 * parity

    def at_y(step):
        return lax.rem(y + (step + NY) % NY, NY)

    def at_x(step):
        return lax.rem(x + (step + NX) % NX, NX)

    def at_zh(step):
        return lax.rem(zh + (step + NZH) % NZH, NZH)

    def dev(yy=y, zz=zl, kk=k, xx=x, hh=zh):
        return {"context": (yy * NZL + zz) * NK + kk, "tensor": xx * NZH + hh}

    zls = (zl, ozl)
    far = [(s, o) for s in range(NY) for o in range(2) if (s, o) != (0, 0)]
    core_peer = dev(kk=ok)
    right, left = dev(yy=at_y(1)), dev(yy=at_y(-1))

    recv_names, send_names = {}, {}

    steps = (0, 1, 7, 2, 6, 3, 5, 4)
    parts = ((0, 3), (3, 5), (5, 8))

    def send(name, src, dst, to, group=None):
        slot = recv_names.setdefault(name, len(recv_names))
        group = name if group is None else group
        sent = send_names.setdefault(group, len(send_names))
        pltpu.make_async_remote_copy(
            src_ref=src, dst_ref=dst, send_sem=send_sems.at[sent], recv_sem=recv_sems.at[slot],
            device_id=to, device_id_type=pl.DeviceIdType.MESH,
        ).start()
        pending.setdefault(group, src)

    def arrived(name, dst):
        slot = recv_names.setdefault(name, len(recv_names))
        pltpu.make_async_copy(dst, dst, recv_sems.at[slot]).wait()

    pending = {}

    def drain():
        for group, src in pending.items():
            pltpu.make_async_copy(src, src, send_sems.at[send_names[group]]).wait()
        pending.clear()

    peers = [dev(yy=at_y(s), zz=zls[o]) for s, o in far]
    peers += [dev(hh=at_zh(s)) for s in range(1, NZH)]
    peers += [dev(xx=at_x(s)) for s in range(1, NX)]
    peers += [dev(xx=at_x(s), hh=ozh) for s in range(1, NX)]
    peers += [core_peer]
    barrier = pltpu.get_barrier_semaphore()
    for peer in peers:
        pl.semaphore_signal(barrier, inc=1, device_id=peer, device_id_type=pl.DeviceIdType.MESH)

    def goes(hop, o, right_way, piece):
        return hop < 4 or (hop == 4 and right_way == ((piece in (0, 1, 2)) == (o == 0)))

    def ring_send(kind, buf, hop, o, at, piece):
        for right_way in (True, False):
            if goes(hop, o, right_way, piece):
                ref = buf.at[at_y(1 - hop if right_way else hop - 1), k, zls[o]].at[at]
                name = (kind + ("r" if right_way else "l"), hop, o, piece)
                send(name, ref, ref, right if right_way else left, kind + "ring")

    def ring_q(hop, o, s):
        ring_send("q", gq, hop, o, s, s)

    def ring_v(hop, o):
        ring_send("v", gv, hop, o, pl.ds(0, NX), "v")

    def cross(kind, buf, at, piece):
        ref = buf.at[y, k, zl].at[at]
        send((kind + "z", piece), ref, ref, dev(zz=ozl), kind + "z")

    def start_q(s):
        ring_q(1, 0, s)
        cross("q", gq, s, s)

    def to_core(kind, buf, step, o):
        ref = buf.at[at_y(step), k, zls[o]]
        send(("k", step), ref, ref, core_peer, kind + "k")

    loads[2].wait()
    loads[3].wait()
    gq[y, k, zl, 0] = qc_ref[pl.ds(pl.multiple_of(32 * x, 32), 32), :]
    for j in range(NX):
        part = kvc_ref[32 * j:32 * j + 32, :]
        keys, values = part[:, :128], part[:, 128:]
        va[j] = jnp.where(parity == 0, keys, values)
        ks[j] = jnp.where(parity == 0, values, keys)
    pl.semaphore_wait(barrier, len(peers))
    start_q(0)
    for s in (2, 1, 3):
        there = at_x(s)
        send(("qa", s), qc_ref.at[pl.ds(pl.multiple_of(32 * there, 32), 32)], gq.at[y, k, zl, s], dev(xx=there), "qa")
    for s in (2, 1, 3):
        send(("kb", s), ks.at[at_x(s)], kb.at[s], dev(xx=at_x(s), hh=ozh), "kb")
        send(("ka", s), va.at[at_x(s)], ka.at[s], dev(xx=at_x(s)), "ka")
    send(("kb", 0), ks.at[x], kb.at[0], dev(hh=ozh), "kb")
    ka[0] = va[x]

    loads[0].wait()
    loads[1].wait()
    rows = x_ref[...].astype(F32)
    inv = lax.rsqrt(jnp.mean(rows * rows, axis=-1, keepdims=True) + 1e-06)
    for b in range(NY * NZL):
        both = []
        for j in (0, 1):
            cols = slice((2 * b + j) * 256, (2 * b + j + 1) * 256)
            unit = rows[:, cols] * inv
            both.append((unit * gain_ref[:, cols]).astype(BF16).astype(F32))
        xk_keep[b] = jnp.where(k == 0, both[0], both[1])
        xk_send[b] = jnp.where(k == 0, both[1], both[0])
    send("xk", xk_send, xk_recv, core_peer)

    loads[4].wait()
    loads[5].wait()
    wb[0, :, :128] = kvw_ref[...]
    wb[0, :, 128:] = qw_ref[...]
    send("w_right", wb.at[0], wb.at[1], dev(xx=at_x(1)), "w")
    send("w_left", wb.at[0], wb.at[3], dev(xx=at_x(-1)), "w")

    arrived("xk", xk_recv)
    for b in range(NY * NZL):
        keep, recv = xk_keep[b], xk_recv[b]
        pair = [jnp.where(k == 0, keep, recv), jnp.where(k == 0, recv, keep)]
        xb[b] = jnp.concatenate(pair, axis=0).astype(BF16)
    for s, o in far:
        there = steps.index((-s) % NY)
        send(("xa", [first <= there < last for first, last in parts].index(True)), xb.at[at_y(s) * NZL + zls[o]], xg.at[zh, there, zl], dev(yy=at_y(s), zz=zls[o]), "xa")
    pending["xa"] = xb.at[pl.ds(0, 15)]
    xg[zh, 0, zl] = xb[y * NZL + zl]

    for s in (1, 3, 2):
        arrived(("qa", s), gq.at[y, k, zl, s])
        start_q(s)
    to_core("q", gq, 0, 0)

    def pass_on(kind, buf, hop, o, at, piece):
        steps = [step for step in ((-hop, hop) if hop < 4 else (4,))]
        for step in steps:
            right_way = goes(hop, o, True, piece) if hop == 4 else step < 0
            arrived((kind + ("r" if right_way else "l"), hop, o, piece), buf.at[at_y(step), k, zls[o]].at[at])
        ring_send(kind, buf, hop + 1, o, at, piece)

    def rows_part(p):
        first, last = parts[p]
        arrived(("xa", p), xb.at[pl.ds(0, 2 * (last - first) - (p == 0))])
        at = xg.at[zh, pl.ds(first, last - first)]
        send(("x_right", p), at, at, dev(hh=at_zh(1)), "x")
        send(("x_left", p), at, at, dev(hh=at_zh(-1)), "x")

    def rows_far(p):
        first, last = parts[p]
        for name, step, z, to in (("x_right", -1, 0, 1), ("x_left", 1, 1, -1)):
            arrived((name, p), xg.at[at_zh(step), pl.ds(first, last - first)])
            at = xg.at[at_zh(step), pl.ds(first, last - first), z]
            send((name, p, "far"), at, at, dev(hh=at_zh(to)), "x")

    def hop_core(kind, buf, hop, o):
        if 0 < hop < 4:
            to_core(kind, buf, -hop, o)
        to_core(kind, buf, hop, o)

    def hop_q(hop, o):
        for s in (0, 1, 3, 2):
            pass_on("q", gq, hop, o, s, s)
        hop_core("q", gq, hop, o)

    def hop_v(hop, o):
        pass_on("v", gv, hop, o, pl.ds(0, NX), "v")
        hop_core("v", gv, hop, o)

    def crossed_q():
        for s in (0, 1, 3, 2):
            arrived(("qz", s), gq.at[y, k, ozl, s])
            ring_q(1, 1, s)
        to_core("q", gq, 0, 1)

    def crossed_v():
        arrived(("vz", "v"), gv.at[y, k, ozl])
        ring_v(1, 1)
        to_core("v", gv, 0, 1)

    def pair_heads():
        for s in range(NX):
            if s:
                arrived(("ka", s), ka.at[s])
            arrived(("kb", s), kb.at[s])
        gv[y, k, zl] = (ka[...].astype(F32) + kb[...].astype(F32)).astype(BF16)
        ring_v(1, 0)
        cross("v", gv, pl.ds(0, NX), "v")
        to_core("v", gv, 0, 0)

    def normed_grad_terms(step):
        yy = at_y(step)
        arrived(("k", step), gq.at[pl.ds(0, 3), 0, 0])
        acc = jnp.zeros((128, 256), F32)
        for j in range(NX):
            acc += lax.dot_general(
                gq[yy, :, :, j].reshape(128, 256), wb[j, :, 128:], (((1,), (1,)), ((), ())), preferred_element_type=F32
            )
            acc += lax.dot_general(
                gv[yy, :, :, j].reshape(128, 128), wb[j, :, :128], (((1,), (1,)), ((), ())), preferred_element_type=F32
            )
        for h in range(NZH):
            for z in range(NZL):
                start = z * 32 + h * 8
                pb[yy, h, z] = jnp.concatenate([acc[start:start + 8], acc[64 + start:72 + start]], axis=0).astype(BF16)
        for s in (2, 1, 3):
            send(("p", step), pb.at[yy, at_zh(s)], pr.at[yy, zh], dev(hh=at_zh(s)), "p")

    def normed_grad_sum(step):
        yy = at_y(step)
        arrived(("p", step), pr.at[yy, pl.ds(0, 3)])
        total = pb[yy, zh].astype(F32)
        for s in (1, 2, 3):
            total += pr[yy, at_zh(s)].astype(F32)
        fb[yy] = total.astype(BF16)
        for o in (0, 1):
            if (step, o) != (0, 0):
                send(("f", step % NY), fb.at[yy, zls[o]], fr.at[y, zl], dev(yy=yy, zz=zls[o]), "f")
        if step == 0:
            fr[y, zl] = fb[y, zl]

    pair_heads()
    rows_part(0)
    hop_q(1, 0)
    crossed_q()

    arrived("w_right", wb.at[1])
    send("w_far0", wb.at[1, pl.ds(0, 128)], wb.at[2, pl.ds(0, 128)], dev(xx=at_x(1)), "w")
    arrived("w_left", wb.at[3])
    send("w_far1", wb.at[3, pl.ds(128, 128)], wb.at[2, pl.ds(128, 128)], dev(xx=at_x(-1)), "w")

    rows_part(1)
    hop_v(1, 0)
    crossed_v()
    rows_part(2)
    hop_q(2, 0)
    hop_q(1, 1)
    rows_far(0)
    hop_v(2, 0)
    hop_v(1, 1)

    arrived("w_far0", wb.at[2, pl.ds(0, 128)])
    arrived("w_far1", wb.at[2, pl.ds(128, 128)])
    normed_grad_terms(0)
    hop_q(3, 0)
    hop_q(2, 1)
    rows_far(1)
    normed_grad_terms(-1)
    hop_v(3, 0)
    hop_v(2, 1)
    rows_far(2)
    normed_grad_terms(1)
    hop_q(4, 0)
    hop_q(3, 1)
    hop_v(4, 0)
    normed_grad_terms(-2)
    hop_v(3, 1)
    normed_grad_terms(2)
    hop_q(4, 1)

    normed_grad_terms(-3)
    normed_grad_terms(3)
    hop_v(4, 1)
    pending["qk"], pending["vk"] = gq.at[:, 0], gv.at[:, 0]
    pending["qz"], pending["vz"] = gq.at[0, 0, 0], gv.at[0, 0, 0]
    pending["qring"], pending["vring"] = gq.at[pl.ds(0, 7), 0], gv.at[pl.ds(0, 7), 0]
    pending["w"], pending["x"] = wb.at[pl.ds(0, 3)], xg.at[pl.ds(0, 3)]
    pending["qa"], pending["ka"], pending["kb"] = gq.at[0, 0, 0, pl.ds(0, 3)], va.at[pl.ds(0, 3)], ks
    normed_grad_terms(4)
    pending["p"] = pb.at[:, pl.ds(0, 3)]

    for p, (first, last) in enumerate(parts):
        for name, z in (("x_right", 0), ("x_left", 1)):
            arrived((name, p, "far"), xg.at[at_zh(2), pl.ds(first, last - first), z])

    def turn(n, yy):
        tiles = [[xg[h, n, z].astype(F32) for z in range(NZL)] for h in range(NZH)]
        order = [tiles[h][z][8 * c:8 * c + 8] for c in range(NK) for z in range(NZL) for h in range(NZH)]
        xt[:, pl.ds(pl.multiple_of(yy * 128, 128), 128)] = jnp.concatenate(order, axis=0).T.astype(BF16)

    for n, step in enumerate(steps):
        turn(n, at_y(step))

    def weight_grad(slot, out):
        value = jnp.dot(xt[...], gv[:, :, :, slot].reshape(1024, 128), preferred_element_type=F32)
        out[:, :128] = value.astype(out.dtype)
        query = jnp.dot(xt[...], gq[:, :, :, slot].reshape(1024, 256), preferred_element_type=F32)
        out[:, 128:] = query.astype(out.dtype)

    x1, x3 = at_x(1), at_x(-1)
    weight_grad(2, gwp.at[2])
    send("gw_a", gwp.at[2, pl.ds(0, 128)], gw1.at[0], dev(xx=x1), "gw")
    send("gw_b", gwp.at[2, pl.ds(128, 128)], gw1.at[1], dev(xx=x3), "gw")
    weight_grad(3, gwp.at[3])
    send("gw_c", gwp.at[3, pl.ds(128, 128)], gw2.at[0, 1], dev(xx=x1), "gw")
    weight_grad(1, gwp.at[1])
    send("gw_d", gwp.at[1, pl.ds(0, 128)], gw2.at[1, 0], dev(xx=x3), "gw")
    for step in (0, -1, 1, -2, 2):
        normed_grad_sum(step)
    normed_grad_sum(-3)
    normed_grad_sum(3)
    normed_grad_sum(4)
    pending["f"] = xb.at[pl.ds(0, 15)]
    arrived("gw_a", gw1.at[0])
    gws[0] = (gwp[3, 0:128].astype(F32) + gw1[0].astype(F32)).astype(BF16)
    send("gw_e", gws.at[0], gw2.at[0, 0], dev(xx=x1), "gw")
    arrived("gw_b", gw1.at[1])
    gws[1] = (gwp[1, 128:256].astype(F32) + gw1[1].astype(F32)).astype(BF16)
    send("gw_f", gws.at[1], gw2.at[1, 1], dev(xx=x3), "gw")
    weight_grad(0, gw_own)
    stores = [pltpu.make_async_copy(gw_own, own_hbm, store_sems.at[1])]
    stores[0].start()

    def swap_cores(n):
        step = steps[n]
        arrived(("f", step), fr.at[0] if step else fr.at[0, 0])
        for o in (0, 1):
            at = fr.at[at_y(-step), zls[o]]
            tile = at[...].astype(F32)
            fk_keep[n, zls[o]] = jnp.where(k == 0, tile[:8], tile[8:])
            fk_send[n, zls[o]] = jnp.where(k == 0, tile[8:], tile[:8])
        there = dn_hbm.at[at_y(-step), :, k]
        send("fk", fk_send.at[n], there, core_peer)
        pltpu.make_async_copy(fk_keep.at[n], there, store_sems.at[0]).start()

    del pending["gw"]
    drain()
    pending["gw"] = gwp.at[pl.ds(0, 3)]
    for n in range(5):
        swap_cores(n)
    for n in range(5, 8):
        swap_cores(n)
    pending["fk"] = fk_send
    drain()
    stores[0].wait()
    pltpu.make_async_copy(fk_keep, fk_keep, store_sems.at[0]).wait()
    arrived("fk", fk_send)
    arrived("gw_c", gw2.at[0, 1])
    arrived("gw_d", gw2.at[1, 0])
    arrived("gw_e", gw2.at[0, 0])
    arrived("gw_f", gw2.at[1, 1])
    assert (len(send_names), len(recv_names)) == (N_SEND, N_RECV), (len(send_names), len(recv_names))


def finish(x_ref, gain_ref, dn_ref, own_ref, gw_ref, dx_ref, gkv_ref, gq_ref):
    for half in (0, 1):
        at = slice(128 * half, 128 * half + 128)
        total = own_ref[at] + gw_ref[0, half].astype(F32) + gw_ref[1, half].astype(F32)
        gkv_ref[at] = total[:, :128]
        gq_ref[at] = total[:, 128:]
    rows = x_ref[...].astype(F32)
    inv = lax.rsqrt(jnp.mean(rows * rows, axis=-1, keepdims=True) + 1e-06)
    dot = jnp.zeros((8, 256), F32)
    blocks = []
    for b in range(NY * NZL * NK):
        cols = slice(256 * b, 256 * b + 256)
        scaled = gain_ref[:, cols] * dn_ref[b // 4, b // 2 % 2, b % 2]
        unit = rows[:, cols] * inv
        dot += scaled * unit
        blocks.append((cols, scaled, unit))
    mean = jnp.sum(dot, axis=-1, keepdims=True) * (1.0 / 8192)
    for cols, scaled, unit in blocks:
        dx_ref[:, cols] = (inv * (scaled - unit * mean)).astype(BF16)


def on_device(block_input, norm_scale_weight, kv_weight, q_weight, kv_cotangent, q_cotangent):
    hbm = pl.BlockSpec(memory_space=pltpu.HBM)
    vmem = pl.BlockSpec(memory_space=pltpu.VMEM)

    def buf(dtype, *shape):
        return pltpu.VMEM(shape, dtype)

    gain = norm_scale_weight.reshape(1, -1)
    dn, own, gw2 = pl.pallas_call(
        kernel,
        out_shape=(
            jax.ShapeDtypeStruct((NY, NZL, NK, 8, 256), F32),
            jax.ShapeDtypeStruct((256, 384), F32),
            jax.ShapeDtypeStruct((2, 2, 128, 384), BF16),
        ),
        in_specs=[hbm] * 6,
        out_specs=(hbm,) * 3,
        scratch_shapes=[
            buf(BF16, 8, 8192), buf(F32, 1, 8192), buf(BF16, 256, 128), buf(BF16, 256, 256),
            buf(BF16, 128, 256), buf(BF16, 128, 256),
            buf(F32, 16, 8, 256), buf(F32, 16, 8, 256), buf(F32, 16, 8, 256),
            buf(BF16, 16, 16, 256), buf(BF16, 4, 8, 2, 16, 256), buf(BF16, 256, 1024),
            buf(BF16, 4, 256, 384), buf(BF16, 4, 32, 128), buf(BF16, 4, 32, 128),
            buf(BF16, 4, 32, 128), buf(BF16, 4, 32, 128),
            buf(BF16, 8, 2, 2, 4, 32, 256), buf(BF16, 8, 2, 2, 4, 32, 128),
            buf(BF16, 8, 4, 2, 16, 256), buf(BF16, 8, 4, 2, 16, 256),
            buf(BF16, 8, 2, 16, 256), buf(BF16, 8, 2, 16, 256),
            buf(F32, 8, 2, 8, 256), buf(F32, 8, 2, 8, 256),
            buf(BF16, 4, 256, 384), buf(F32, 256, 384), buf(BF16, 2, 128, 384),
            buf(BF16, 2, 128, 384),
            pltpu.SemaphoreType.DMA((6,)), pltpu.SemaphoreType.DMA((2,)),
            pltpu.SemaphoreType.DMA((N_SEND,)), pltpu.SemaphoreType.DMA((N_RECV,)),
        ],
        compiler_params=pltpu.CompilerParams(
            collective_id=0, has_side_effects=True, vmem_limit_bytes=VL
        ),
        cost_estimate=pl.CostEstimate(flops=1_700_000_000, bytes_accessed=2_000_000, transcendentals=16),
        name="qkv_backward",
    )(
        block_input, gain, kv_weight, q_weight,
        kv_cotangent.reshape(kv_cotangent.shape[0], -1), q_cotangent,
    )
    return pl.pallas_call(
        finish,
        out_shape=(
            jax.ShapeDtypeStruct((8, 8192), BF16),
            jax.ShapeDtypeStruct((256, 128), F32),
            jax.ShapeDtypeStruct((256, 256), F32),
        ),
        in_specs=[vmem] * 5,
        out_specs=(vmem,) * 3,
        compiler_params=pltpu.CompilerParams(vmem_limit_bytes=VL),
        name="finish",
    )(block_input, gain, dn, own, gw2)


def solution(mesh):
    in_specs = (
        P(("context", "tensor"), None),
        P(),
        P("context", "tensor"),
        P("context", "tensor"),
        P("context", "tensor", None),
        P("context", "tensor"),
    )
    out_specs = (P(("context", "tensor"), None), P("context", "tensor"), P("context", "tensor"))
    return jax.shard_map(
        on_device, mesh=mesh, in_specs=in_specs, out_specs=out_specs, check_vma=False
    )
```

```python
import jax
import jax.numpy as jnp
from jax import lax
from jax.experimental import pallas as pl
from jax.experimental.pallas import tpu as pltpu
from jax.sharding import PartitionSpec as P

NY, NZL, NK = 8, 2, 2
NX, NZH = 4, 4
F32, BF16 = jnp.float32, jnp.bfloat16
N_SEND, N_RECV = 17, 120
VL = 63_400_000


def kernel(
    x_hbm, gain_hbm, kvw_hbm, qw_hbm, kvc_hbm, qc_hbm,
    dn_hbm, own_hbm, gw2,
    x_ref, gain_ref, kvw_ref, qw_ref, kvc_ref, qc_ref,
    xk_keep, xk_send, xk_recv, xb, xg, xt,
    wb, va, ka, ks, kb, gq, gv,
    pb, pr, fb, fr, fk_keep, fk_send,
    gwp, gw_own, gw1, gws,
    load_sems, store_sems, send_sems, recv_sems,
):
    loads = [
        pltpu.make_async_copy(src, dst, load_sems.at[i])
        for i, (src, dst) in enumerate([
            (x_hbm, x_ref), (gain_hbm, gain_ref), (qc_hbm, qc_ref),
            (kvc_hbm, kvc_ref), (kvw_hbm, kvw_ref), (qw_hbm, qw_ref),
        ])
    ]
    for load in loads:
        load.start()

    context = lax.axis_index("context")
    tensor = lax.axis_index("tensor")
    y, zl, k = lax.div(context, NZL * NK), lax.rem(lax.div(context, NK), NZL), lax.rem(context, NK)
    x, zh = lax.div(tensor, NZH), lax.rem(tensor, NZH)
    ozl, ok = 1 - zl, 1 - k
    parity = lax.rem(zh, 2)
    ozh = zh + 1 - 2 * parity

    def at_y(step):
        return lax.rem(y + (step + NY) % NY, NY)

    def at_x(step):
        return lax.rem(x + (step + NX) % NX, NX)

    def at_zh(step):
        return lax.rem(zh + (step + NZH) % NZH, NZH)

    def dev(yy=y, zz=zl, kk=k, xx=x, hh=zh):
        return {"context": (yy * NZL + zz) * NK + kk, "tensor": xx * NZH + hh}

    zls = (zl, ozl)
    far = [(s, o) for s in range(NY) for o in range(2) if (s, o) != (0, 0)]
    core_peer = dev(kk=ok)
    right, left = dev(yy=at_y(1)), dev(yy=at_y(-1))

    recv_names, send_names = {}, {}

    steps = (0, 1, 7, 2, 6, 3, 5, 4)
    parts = ((0, 5), (5, 8))

    def send(name, src, dst, to, group=None):
        slot = recv_names.setdefault(name, len(recv_names))
        group = name if group is None else group
        sent = send_names.setdefault(group, len(send_names))
        pltpu.make_async_remote_copy(
            src_ref=src, dst_ref=dst, send_sem=send_sems.at[sent], recv_sem=recv_sems.at[slot],
            device_id=to, device_id_type=pl.DeviceIdType.MESH,
        ).start()
        pending.setdefault(group, src)

    def arrived(name, dst):
        slot = recv_names.setdefault(name, len(recv_names))
        pltpu.make_async_copy(dst, dst, recv_sems.at[slot]).wait()

    pending = {}

    def drain():
        for group, src in pending.items():
            pltpu.make_async_copy(src, src, send_sems.at[send_names[group]]).wait()
        pending.clear()

    peers = [dev(yy=at_y(s), zz=zls[o]) for s, o in far]
    peers += [dev(hh=at_zh(s)) for s in range(1, NZH)]
    peers += [dev(xx=at_x(s)) for s in range(1, NX)]
    peers += [dev(xx=at_x(s), hh=ozh) for s in range(1, NX)]
    peers += [core_peer]
    barrier = pltpu.get_barrier_semaphore()
    for peer in peers:
        pl.semaphore_signal(barrier, inc=1, device_id=peer, device_id_type=pl.DeviceIdType.MESH)

    def goes(hop, o, right_way, piece):
        return hop < 4 or (hop == 4 and right_way == ((piece in (0, 1, 2)) == (o == 0)))

    def ring_send(kind, buf, hop, o, at, piece):
        for right_way in (True, False):
            if goes(hop, o, right_way, piece):
                ref = buf.at[at_y(1 - hop if right_way else hop - 1), k, zls[o]].at[at]
                name = (kind + ("r" if right_way else "l"), hop, o, piece)
                send(name, ref, ref, right if right_way else left, kind + "ring")

    def ring_q(hop, o, s):
        ring_send("q", gq, hop, o, s, s)

    def ring_v(hop, o):
        ring_send("v", gv, hop, o, pl.ds(0, NX), "v")

    def cross(kind, buf, at, piece):
        ref = buf.at[y, k, zl].at[at]
        send((kind + "z", piece), ref, ref, dev(zz=ozl), kind + "z")

    def start_q(s):
        ring_q(1, 0, s)
        cross("q", gq, s, s)

    def to_core(kind, buf, step, o):
        ref = buf.at[at_y(step), k, zls[o]]
        send(("k", step), ref, ref, core_peer, kind + "k")

    loads[2].wait()
    loads[3].wait()
    gq[y, k, zl, 0] = qc_ref[pl.ds(pl.multiple_of(32 * x, 32), 32), :]
    for j in range(NX):
        part = kvc_ref[32 * j:32 * j + 32, :]
        keys, values = part[:, :128], part[:, 128:]
        va[j] = jnp.where(parity == 0, keys, values)
        ks[j] = jnp.where(parity == 0, values, keys)
    pl.semaphore_wait(barrier, len(peers))
    start_q(0)
    for s in (2, 1, 3):
        there = at_x(s)
        send(("qa", s), qc_ref.at[pl.ds(pl.multiple_of(32 * there, 32), 32)], gq.at[y, k, zl, s], dev(xx=there), "qa")
    for s in (2, 1, 3):
        send("kb", ks.at[at_x(s)], kb.at[s], dev(xx=at_x(s), hh=ozh), "kb")
        send("ka", va.at[at_x(s)], ka.at[s], dev(xx=at_x(s)), "ka")
    send("kb", ks.at[x], kb.at[0], dev(hh=ozh), "kb")
    ka[0] = va[x]

    loads[0].wait()
    loads[1].wait()
    rows = x_ref[...].astype(F32)
    inv = lax.rsqrt(jnp.mean(rows * rows, axis=-1, keepdims=True) + 1e-06)
    for b in range(NY * NZL):
        both = []
        for j in (0, 1):
            cols = slice((2 * b + j) * 256, (2 * b + j + 1) * 256)
            unit = rows[:, cols] * inv
            both.append((unit * gain_ref[:, cols]).astype(BF16).astype(F32))
        xk_keep[b] = jnp.where(k == 0, both[0], both[1])
        xk_send[b] = jnp.where(k == 0, both[1], both[0])
    send("xk", xk_send, xk_recv, core_peer)

    loads[4].wait()
    loads[5].wait()
    wb[0, :, :128] = kvw_ref[...]
    wb[0, :, 128:] = qw_ref[...]
    send("w_right", wb.at[0], wb.at[1], dev(xx=at_x(1)), "w")
    send("w_left", wb.at[0], wb.at[3], dev(xx=at_x(-1)), "w")

    arrived("xk", xk_recv)
    for b in range(NY * NZL):
        keep, recv = xk_keep[b], xk_recv[b]
        pair = [jnp.where(k == 0, keep, recv), jnp.where(k == 0, recv, keep)]
        xb[b] = jnp.concatenate(pair, axis=0).astype(BF16)
    for s, o in far:
        there = steps.index((-s) % NY)
        send(("xa", [first <= there < last for first, last in parts].index(True)), xb.at[at_y(s) * NZL + zls[o]], xg.at[zh, there, zl], dev(yy=at_y(s), zz=zls[o]), "xa")
    pending["xa"] = xb.at[pl.ds(0, 15)]
    xg[zh, 0, zl] = xb[y * NZL + zl]

    for s in (1, 3, 2):
        arrived(("qa", s), gq.at[y, k, zl, s])
        start_q(s)
    to_core("q", gq, 0, 0)

    def pass_on(kind, buf, hop, o, at, piece):
        steps = [step for step in ((-hop, hop) if hop < 4 else (4,))]
        for step in steps:
            right_way = goes(hop, o, True, piece) if hop == 4 else step < 0
            arrived((kind + ("r" if right_way else "l"), hop, o, piece), buf.at[at_y(step), k, zls[o]].at[at])
        ring_send(kind, buf, hop + 1, o, at, piece)

    def rows_part(p):
        first, last = parts[p]
        arrived(("xa", p), xb.at[pl.ds(0, 2 * (last - first) - (p == 0))])
        at = xg.at[zh, pl.ds(first, last - first)]
        send(("x_right", p), at, at, dev(hh=at_zh(1)), "x")
        send(("x_left", p), at, at, dev(hh=at_zh(-1)), "x")

    def rows_far(p):
        first, last = parts[p]
        for name, step, z, to in (("x_right", -1, 0, 1), ("x_left", 1, 1, -1)):
            arrived((name, p), xg.at[at_zh(step), pl.ds(first, last - first)])
            at = xg.at[at_zh(step), pl.ds(first, last - first), z]
            send(("far", p), at, at, dev(hh=at_zh(to)), "x")

    def hop_core(kind, buf, hop, o):
        if 0 < hop < 4:
            to_core(kind, buf, -hop, o)
        to_core(kind, buf, hop, o)

    def hop_q(hop, o):
        for s in (0, 1, 3, 2):
            pass_on("q", gq, hop, o, s, s)
        hop_core("q", gq, hop, o)

    def hop_v(hop, o):
        pass_on("v", gv, hop, o, pl.ds(0, NX), "v")
        hop_core("v", gv, hop, o)

    def crossed_q():
        for s in (0, 1, 3, 2):
            arrived(("qz", s), gq.at[y, k, ozl, s])
            ring_q(1, 1, s)
        to_core("q", gq, 0, 1)

    def crossed_v():
        arrived(("vz", "v"), gv.at[y, k, ozl])
        ring_v(1, 1)
        to_core("v", gv, 0, 1)

    def pair_heads():
        arrived("ka", ka.at[pl.ds(1, 3)])
        arrived("kb", kb)
        gv[y, k, zl] = (ka[...].astype(F32) + kb[...].astype(F32)).astype(BF16)
        ring_v(1, 0)
        cross("v", gv, pl.ds(0, NX), "v")
        to_core("v", gv, 0, 0)

    def normed_grad_terms(step):
        yy = at_y(step)
        arrived(("k", step), gq.at[pl.ds(0, 3), 0, 0])
        acc = jnp.zeros((128, 256), F32)
        for j in range(NX):
            acc += lax.dot_general(
                gq[yy, :, :, j].reshape(128, 256), wb[j, :, 128:], (((1,), (1,)), ((), ())), preferred_element_type=F32
            )
            acc += lax.dot_general(
                gv[yy, :, :, j].reshape(128, 128), wb[j, :, :128], (((1,), (1,)), ((), ())), preferred_element_type=F32
            )
        for h in range(NZH):
            for z in range(NZL):
                start = z * 32 + h * 8
                pb[yy, h, z] = jnp.concatenate([acc[start:start + 8], acc[64 + start:72 + start]], axis=0).astype(BF16)
        for s in (2, 1, 3):
            send(("p", step), pb.at[yy, at_zh(s)], pr.at[yy, zh], dev(hh=at_zh(s)), "p")

    def normed_grad_sum(step):
        yy = at_y(step)
        arrived(("p", step), pr.at[yy, pl.ds(0, 3)])
        total = pb[yy, zh].astype(F32)
        for s in (1, 2, 3):
            total += pr[yy, at_zh(s)].astype(F32)
        fb[yy] = total.astype(BF16)
        for o in (0, 1):
            if (step, o) != (0, 0):
                send(("f", step % NY), fb.at[yy, zls[o]], fr.at[y, zl], dev(yy=yy, zz=zls[o]), "f")
        if step == 0:
            fr[y, zl] = fb[y, zl]

    pair_heads()
    rows_part(0)
    hop_q(1, 0)
    crossed_q()

    arrived("w_right", wb.at[1])
    send("w_far", wb.at[1, pl.ds(0, 128)], wb.at[2, pl.ds(0, 128)], dev(xx=at_x(1)), "w")
    arrived("w_left", wb.at[3])
    send("w_far", wb.at[3, pl.ds(128, 128)], wb.at[2, pl.ds(128, 128)], dev(xx=at_x(-1)), "w")

    hop_v(1, 0)
    crossed_v()
    rows_part(1)
    hop_q(2, 0)
    hop_q(1, 1)
    rows_far(0)
    hop_v(2, 0)
    hop_v(1, 1)

    arrived("w_far", wb.at[2])
    normed_grad_terms(0)
    hop_q(3, 0)
    hop_q(2, 1)
    normed_grad_terms(-1)
    hop_v(3, 0)
    hop_v(2, 1)
    rows_far(1)
    normed_grad_terms(1)
    hop_q(4, 0)
    hop_q(3, 1)
    hop_v(4, 0)
    normed_grad_terms(-2)
    hop_v(3, 1)
    normed_grad_terms(2)
    hop_q(4, 1)

    normed_grad_terms(-3)
    normed_grad_terms(3)
    hop_v(4, 1)
    pending["qk"], pending["vk"] = gq.at[:, 0], gv.at[:, 0]
    pending["qz"], pending["vz"] = gq.at[0, 0, 0], gv.at[0, 0, 0]
    pending["qring"], pending["vring"] = gq.at[pl.ds(0, 7), 0], gv.at[pl.ds(0, 7), 0]
    pending["w"], pending["x"] = wb.at[pl.ds(0, 3)], xg.at[pl.ds(0, 3)]
    pending["qa"], pending["ka"], pending["kb"] = gq.at[0, 0, 0, pl.ds(0, 3)], va.at[pl.ds(0, 3)], ks
    normed_grad_terms(4)
    pending["p"] = pb.at[:, pl.ds(0, 3)]

    for p, (first, last) in enumerate(parts):
        arrived(("far", p), xg.at[at_zh(2), pl.ds(first, last - first)])

    def turn(n, yy):
        tiles = [[xg[h, n, z].astype(F32) for z in range(NZL)] for h in range(NZH)]
        order = [tiles[h][z][8 * c:8 * c + 8] for c in range(NK) for z in range(NZL) for h in range(NZH)]
        xt[:, pl.ds(pl.multiple_of(yy * 128, 128), 128)] = jnp.concatenate(order, axis=0).T.astype(BF16)

    for n, step in enumerate(steps):
        turn(n, at_y(step))

    def weight_grad(slot, out):
        value = jnp.dot(xt[...], gv[:, :, :, slot].reshape(1024, 128), preferred_element_type=F32)
        out[:, :128] = value.astype(out.dtype)
        query = jnp.dot(xt[...], gq[:, :, :, slot].reshape(1024, 256), preferred_element_type=F32)
        out[:, 128:] = query.astype(out.dtype)

    x1, x3 = at_x(1), at_x(-1)
    weight_grad(2, gwp.at[2])
    send("gw_a", gwp.at[2, pl.ds(0, 128)], gw1.at[0], dev(xx=x1), "gw")
    send("gw_b", gwp.at[2, pl.ds(128, 128)], gw1.at[1], dev(xx=x3), "gw")
    weight_grad(3, gwp.at[3])
    send("gw2", gwp.at[3, pl.ds(128, 128)], gw2.at[0, 1], dev(xx=x1), "gw")
    weight_grad(1, gwp.at[1])
    send("gw2", gwp.at[1, pl.ds(0, 128)], gw2.at[1, 0], dev(xx=x3), "gw")
    for step in (0, -1, 1, -2, 2):
        normed_grad_sum(step)
    normed_grad_sum(-3)
    normed_grad_sum(3)
    normed_grad_sum(4)
    pending["f"] = xb.at[pl.ds(0, 15)]
    arrived("gw_a", gw1.at[0])
    gws[0] = (gwp[3, 0:128].astype(F32) + gw1[0].astype(F32)).astype(BF16)
    send("gw2", gws.at[0], gw2.at[0, 0], dev(xx=x1), "gw")
    arrived("gw_b", gw1.at[1])
    gws[1] = (gwp[1, 128:256].astype(F32) + gw1[1].astype(F32)).astype(BF16)
    send("gw2", gws.at[1], gw2.at[1, 1], dev(xx=x3), "gw")
    weight_grad(0, gw_own)
    stores = [pltpu.make_async_copy(gw_own, own_hbm, store_sems.at[1])]
    stores[0].start()

    def swap_cores(n):
        step = steps[n]
        arrived(("f", step), fr.at[0] if step else fr.at[0, 0])
        for o in (0, 1):
            at = fr.at[at_y(-step), zls[o]]
            tile = at[...].astype(F32)
            fk_keep[n, zls[o]] = jnp.where(k == 0, tile[:8], tile[8:])
            fk_send[n, zls[o]] = jnp.where(k == 0, tile[8:], tile[:8])
        there = dn_hbm.at[at_y(-step), :, k]
        send("fk", fk_send.at[n], there, core_peer)
        pltpu.make_async_copy(fk_keep.at[n], there, store_sems.at[0]).start()

    del pending["gw"]
    drain()
    pending["gw"] = gwp.at[pl.ds(0, 3)]
    for n in range(5):
        swap_cores(n)
    for n in range(5, 8):
        swap_cores(n)
    pending["fk"] = fk_send
    drain()
    stores[0].wait()
    pltpu.make_async_copy(fk_keep, fk_keep, store_sems.at[0]).wait()
    arrived("fk", fk_send)
    arrived("gw2", gw2)
    assert (len(send_names), len(recv_names)) == (N_SEND, N_RECV), (len(send_names), len(recv_names))


def finish(x_ref, gain_ref, dn_ref, own_ref, gw_ref, dx_ref, gkv_ref, gq_ref):
    for half in (0, 1):
        at = slice(128 * half, 128 * half + 128)
        total = own_ref[at] + gw_ref[0, half].astype(F32) + gw_ref[1, half].astype(F32)
        gkv_ref[at] = total[:, :128]
        gq_ref[at] = total[:, 128:]
    rows = x_ref[...].astype(F32)
    inv = lax.rsqrt(jnp.mean(rows * rows, axis=-1, keepdims=True) + 1e-06)
    dot = jnp.zeros((8, 256), F32)
    blocks = []
    for b in range(NY * NZL * NK):
        cols = slice(256 * b, 256 * b + 256)
        scaled = gain_ref[:, cols] * dn_ref[b // 4, b // 2 % 2, b % 2]
        unit = rows[:, cols] * inv
        dot += scaled * unit
        blocks.append((cols, scaled, unit))
    mean = jnp.sum(dot, axis=-1, keepdims=True) * (1.0 / 8192)
    for cols, scaled, unit in blocks:
        dx_ref[:, cols] = (inv * (scaled - unit * mean)).astype(BF16)


def on_device(block_input, norm_scale_weight, kv_weight, q_weight, kv_cotangent, q_cotangent):
    hbm = pl.BlockSpec(memory_space=pltpu.HBM)
    vmem = pl.BlockSpec(memory_space=pltpu.VMEM)

    def buf(dtype, *shape):
        return pltpu.VMEM(shape, dtype)

    gain = norm_scale_weight.reshape(1, -1)
    dn, own, gw2 = pl.pallas_call(
        kernel,
        out_shape=(
            jax.ShapeDtypeStruct((NY, NZL, NK, 8, 256), F32),
            jax.ShapeDtypeStruct((256, 384), F32),
            jax.ShapeDtypeStruct((2, 2, 128, 384), BF16),
        ),
        in_specs=[hbm] * 6,
        out_specs=(hbm,) * 3,
        scratch_shapes=[
            buf(BF16, 8, 8192), buf(F32, 1, 8192), buf(BF16, 256, 128), buf(BF16, 256, 256),
            buf(BF16, 128, 256), buf(BF16, 128, 256),
            buf(F32, 16, 8, 256), buf(F32, 16, 8, 256), buf(F32, 16, 8, 256),
            buf(BF16, 16, 16, 256), buf(BF16, 4, 8, 2, 16, 256), buf(BF16, 256, 1024),
            buf(BF16, 4, 256, 384), buf(BF16, 4, 32, 128), buf(BF16, 4, 32, 128),
            buf(BF16, 4, 32, 128), buf(BF16, 4, 32, 128),
            buf(BF16, 8, 2, 2, 4, 32, 256), buf(BF16, 8, 2, 2, 4, 32, 128),
            buf(BF16, 8, 4, 2, 16, 256), buf(BF16, 8, 4, 2, 16, 256),
            buf(BF16, 8, 2, 16, 256), buf(BF16, 8, 2, 16, 256),
            buf(F32, 8, 2, 8, 256), buf(F32, 8, 2, 8, 256),
            buf(BF16, 4, 256, 384), buf(F32, 256, 384), buf(BF16, 2, 128, 384),
            buf(BF16, 2, 128, 384),
            pltpu.SemaphoreType.DMA((6,)), pltpu.SemaphoreType.DMA((2,)),
            pltpu.SemaphoreType.DMA((N_SEND,)), pltpu.SemaphoreType.DMA((N_RECV,)),
        ],
        compiler_params=pltpu.CompilerParams(
            collective_id=0, has_side_effects=True, vmem_limit_bytes=VL
        ),
        cost_estimate=pl.CostEstimate(flops=1_700_000_000, bytes_accessed=2_000_000, transcendentals=16),
        name="qkv_backward",
    )(
        block_input, gain, kv_weight, q_weight,
        kv_cotangent.reshape(kv_cotangent.shape[0], -1), q_cotangent,
    )
    return pl.pallas_call(
        finish,
        out_shape=(
            jax.ShapeDtypeStruct((8, 8192), BF16),
            jax.ShapeDtypeStruct((256, 128), F32),
            jax.ShapeDtypeStruct((256, 256), F32),
        ),
        in_specs=[vmem] * 5,
        out_specs=(vmem,) * 3,
        compiler_params=pltpu.CompilerParams(vmem_limit_bytes=VL),
        name="finish",
    )(block_input, gain, dn, own, gw2)


def solution(mesh):
    in_specs = (
        P(("context", "tensor"), None),
        P(),
        P("context", "tensor"),
        P("context", "tensor"),
        P("context", "tensor", None),
        P("context", "tensor"),
    )
    out_specs = (P(("context", "tensor"), None), P("context", "tensor"), P("context", "tensor"))
    return jax.shard_map(
        on_device, mesh=mesh, in_specs=in_specs, out_specs=out_specs, check_vma=False
    )
```
